32 devices in a mesh: span: 4 (over y, x), tok: 8 (over z, core).
Axes of the slice: x: 2, y: 2, z: 4, core: 2. Of those that a mesh axis runs over, the one named last changes fastest.
Arguments:
- latents: bfloat16 [4, 512, 3584], P('span', 'tok'), may hold values from -6 to 6
- levels: int32 [4], P('span'), may hold values from 0 to 14
- visible: int32 [4, 4], replicated, may hold values 0 or 1
- frame_counts: int32 [4], replicated, may hold values from 0 to 2
- modulation: float32 [16, 3, 3584], replicated, may hold values from -4 to 4
- w_qkv: bfloat16 [3584, 3, 4096], P(None, None, 'tok')
- qk_gain: float32 [2, 4096], P(None, 'tok'), may hold values from 0 to 5
- w_out: bfloat16 [4096, 3584], P('tok'), may hold values from -0.09375 to 0.09375
- w_head: bfloat16 [3584, 96], replicated, may hold values from -0.09375 to 0.09375
- conv_w: bfloat16 [3, 96, 384], replicated, may hold values from -0.375 to 0.375
Outputs:
- denoised: bfloat16 [4, 512, 3584], P('span', 'tok')
- decoded: bfloat16 [4, 512, 384], P('span', 'tok')
The draws below stay inside these ranges and needn't reach their ends.
All inputs are finite; a program needn't handle non-finite values.
Results may differ from the reference program's by a relative error of at most 0.015.
Values may be sent and summed in bfloat16 or wider, within the bound.
No kernel may reach another device: no remote copies, remote signals or barrier semaphores. Data moves between devices by JAX's collectives and lax.ppermute only.
A program may use at most 128 MiB of HBM per device.

```python
import jax
import jax.numpy as jnp
from jax import lax

D = 3584
HEADS = 32
HD = 128
CV = 96
CH = 384
FRAMES = 8
LEVELS = 16
KEEP = 2
SPOTS = 8
TOK_DEV = 64
CT = 512
CLIPS = 4
HEADS_DEV = 4
N_TOK = 8


def draw_w_qkv(key, part):
    base = jax.random.normal(key, (D, 3, HEADS * HD), jnp.float32)
    base = jnp.clip(base, -6.0, 6.0) * D ** (-0.5)
    return base.astype(jnp.bfloat16)


def draw_qk_gain(key, part):
    return jax.random.uniform(key, (2, HEADS * HD), jnp.float32, 0.6, 1.6)


def set_ends(drawn, key, low, top_value):
    dims = drawn.shape
    spot = [jax.random.randint(jax.random.fold_in(key, axis), (), 0, dims[axis]) for axis in range(len(dims))]
    drawn = drawn.at[tuple(spot)].set(low)
    longest = dims.index(max(dims))
    spot[longest] = (spot[longest] + 1) % dims[longest]
    return drawn.at[tuple(spot)].set(top_value)


def level_of(stream_key, shape, split, least, top_value):
    loudness = 1.0
    for axis_at, blocks in split:
        steps = jax.random.uniform(jax.random.fold_in(jax.random.fold_in(stream_key, 6), axis_at), (blocks,), jnp.float32, least / len(split), top_value / len(split))
        loudness = loudness * jnp.repeat(jnp.exp(steps), shape[axis_at] // blocks).reshape((-1,) + (1,) * (len(shape) - 1 - axis_at))
    return loudness


def centred(own_key, extent, scale, bound, split=(), kind=jnp.bfloat16):
    factor_of = level_of(own_key, extent, split, -0.22, 0.18) if split else 1.0
    entries = jax.random.normal(own_key, extent, jnp.float32) * scale * factor_of
    return jnp.minimum(jnp.maximum(entries, -bound), bound).astype(kind)


def setup_inputs(seed: int = 0) -> dict:
    splits = jax.random.split(jax.random.key(seed), 11)
    latents = centred(splits[0], (CLIPS, CT, D), 1.0, 6.0, ((0, 4), (1, 8)))
    levels = set_ends(jax.random.randint(splits[1], (CLIPS,), 0, LEVELS - 1), jax.random.fold_in(splits[1], 1), 0, (LEVELS - 1) - 1).astype(jnp.int32)
    visible = set_ends((jax.random.randint(splits[2], (CLIPS, CLIPS), 0, 4) < 3).astype(jnp.int32), jax.random.fold_in(splits[2], 1), 0, 1)
    frame_counts = set_ends(jax.random.randint(splits[3], (CLIPS,), 0, KEEP + 1), jax.random.fold_in(splits[3], 1), 0, KEEP).astype(jnp.int32)
    modulation = centred(splits[4], (LEVELS, 3, D), 1.0, 4.0, (), jnp.float32)
    w_qkv = draw_w_qkv(jax.random.fold_in(splits[10], 71), 0)
    qk_gain = draw_qk_gain(jax.random.fold_in(splits[10], 71), 0)
    w_out = centred(splits[7], (HEADS * HD, D), (HEADS * HD) ** -0.5, 0.09375, ((0, 8),))
    w_head = centred(splits[8], (D, CV), D ** -0.5, 0.09375)
    conv_w = centred(splits[9], (3, CV, CH), (3 * CV) ** -0.5, 0.375)
    return {"latents": latents, "levels": levels, "visible": visible, "frame_counts": frame_counts, "modulation": modulation, "w_qkv": w_qkv, "qk_gain": qk_gain, "w_out": w_out, "w_head": w_head, "conv_w": conv_w}


EPS = 1e-06
NEG = -1e+30

def modulate(rows, shift, scale):
    values = rows.astype(jnp.float32)
    centre = values - lax.optimization_barrier(jnp.mean(values, -1, keepdims=True))
    spread = lax.optimization_barrier(jnp.mean(centre * centre, -1, keepdims=True))
    return (centre * lax.rsqrt(spread + EPS) * (1.0 + scale) + shift).astype(jnp.bfloat16)

def qk_scale(tensor, gain):
    square = lax.optimization_barrier(jnp.mean(tensor * tensor, -1, keepdims=True))
    return (tensor * lax.rsqrt(square + EPS) * gain.reshape(tensor.shape[-2], tensor.shape[-1])).astype(jnp.bfloat16)

def reference(latents, levels, visible, frame_counts, modulation, w_qkv, qk_gain, w_out, w_head, conv_w):
    clip_ids = jnp.arange(CLIPS, dtype=jnp.int32)
    place = jnp.arange(CT, dtype=jnp.int32)
    frame_of = place % TOK_DEV // SPOTS
    key_ok = frame_of[None, :] < frame_counts[:, None]
    w_flat = w_qkv.reshape(D, 3 * HEADS * HD)
    w_groups = w_out.reshape(N_TOK, HEADS_DEV * HD, D)
    state = latents
    table = modulation[levels]
    modulated = modulate(state, table[:, 0][:, None, :], table[:, 1][:, None, :])
    proj = jnp.dot(modulated.reshape(CLIPS * CT, D), w_flat, preferred_element_type=jnp.float32)
    proj = proj.reshape(CLIPS * CT, 3, HEADS, HD)
    query = qk_scale(proj[:, 0], qk_gain[0]).reshape(CLIPS, CT, N_TOK, HEADS_DEV, HD)
    query = query.transpose(0, 2, 1, 3, 4)
    keys = qk_scale(proj[:, 1], qk_gain[1]).reshape(CLIPS * CT, N_TOK, HEADS_DEV, HD).transpose(1, 0, 2, 3)
    values = proj[:, 2].astype(jnp.bfloat16).reshape(CLIPS * CT, N_TOK, HEADS_DEV, HD).transpose(1, 0, 2, 3)

    def per_clip(item):
        query_c, clip, rows_c, gate_c = item
        earlier = (clip_ids < clip) & (visible[clip] == 1)
        usable = ((clip_ids == clip)[:, None] | earlier[:, None] & key_ok).reshape(CLIPS * CT)

        def per_group(group):
            query_g, keys_g, values_g, weight_g = group
            scores = jnp.einsum('qhd,khd->hqk', query_g.astype(jnp.float32), keys_g.astype(jnp.float32)) * HD ** (-0.5)
            scores = jnp.where(usable[None, None, :], scores, NEG)
            best = lax.optimization_barrier(jnp.max(scores, -1, keepdims=True))
            terms = jnp.where(usable[None, None, :], jnp.exp(scores - best), 0.0)
            total = lax.optimization_barrier(jnp.sum(terms, -1))
            rounded = lax.optimization_barrier(terms.astype(jnp.bfloat16)).astype(jnp.float32)
            acc = jnp.einsum('hqk,khd->hqd', rounded, values_g.astype(jnp.float32))
            attended = (acc / total[..., None]).transpose(1, 0, 2).reshape(CT, HEADS_DEV * HD).astype(jnp.bfloat16)
            return jnp.dot(attended, weight_g, preferred_element_type=jnp.float32).astype(jnp.bfloat16)
        parts = lax.map(per_group, (query_c, keys, values, w_groups))
        mixed = lax.optimization_barrier(jnp.sum(lax.optimization_barrier(parts).astype(jnp.float32), 0))
        return (rows_c.astype(jnp.float32) + gate_c * mixed).astype(jnp.bfloat16)
    state = lax.map(per_clip, (query, clip_ids, state, table[:, 2]))
    feats = jnp.dot(state.reshape(CLIPS * CT, D), w_head, preferred_element_type=jnp.float32).astype(jnp.bfloat16)
    feats = feats.reshape(CLIPS, N_TOK, FRAMES, SPOTS, CV).transpose(1, 0, 2, 3, 4).reshape(N_TOK, CLIPS * FRAMES, SPOTS, CV)
    length = CLIPS * FRAMES
    padded = jnp.concatenate([jnp.zeros((N_TOK, 2, SPOTS, CV), jnp.bfloat16), feats], 1)
    conv = jnp.zeros((N_TOK * length * SPOTS, CH), jnp.float32)
    for tap in range(3):
        window = padded[:, 2 - tap:2 - tap + length].reshape(N_TOK * length * SPOTS, CV)
        conv = conv + jnp.dot(window, conv_w[tap], preferred_element_type=jnp.float32)
    decoded = jax.nn.silu(conv).astype(jnp.bfloat16)
    decoded = decoded.reshape(N_TOK, CLIPS, FRAMES, SPOTS, CH).transpose(1, 0, 2, 3, 4).reshape(CLIPS, CT, CH)
    return (state, decoded)
```

```python
import functools

import jax
import jax.numpy as jnp
from jax import lax
from jax.experimental import pallas as pl
from jax.experimental.pallas import tpu as pltpu
from jax.sharding import PartitionSpec as P

HD = 128
FRAMES = 8
KEEP = 2
SPOTS = 8
TOK_DEV = 64
CORES = 2
LEAD = KEEP * SPOTS
HALO = 2 * SPOTS


EPS = 1e-06
NEG = -1e30
LOG2E = 1.4426950408889634
MIB = 1 << 20


def routes(line):
    if line == 4:
        return [
            [([(0, 2), (2, 3), (3, 1), (1, 0)], None)],
            [([(0, 1), (1, 3), (3, 2), (2, 0)], None)],
            [([(1, 2), (2, 1)], None), ([(2, 3), (1, 0)], 0)],
        ]
    return [[([(i, (i + by) % line) for i in range(line)], None)] for by in range(1, line)]


def lanes(pairs):
    return [(a * CORES + c, b * CORES + c) for a, b in pairs for c in range(CORES)]


def back(pairs):
    return [(b, a) for a, b in pairs]


def over_core(array):
    devices = lax.axis_size("tok")
    return lax.ppermute(array, "tok", [(i, i ^ 1) for i in range(devices)])


def from_behind(array, axis, by):
    devices = lax.axis_size(axis)
    pairs = [(i, i + by) for i in range(devices) if 0 <= i + by < devices]
    return lax.ppermute(array, axis, pairs)


def vmem():
    return pl.BlockSpec(memory_space=pltpu.VMEM)


def smem():
    return pl.BlockSpec(memory_space=pltpu.SMEM)


def cost(flops, moved, exps=0):
    return pl.CostEstimate(flops=int(flops), bytes_accessed=int(moved), transcendentals=int(exps))


def level_spec(table):
    return pl.BlockSpec((3, 8, table.shape[2]), lambda i, level: (0, level[0] // 8, 0))


def modulate_kernel(level, rows, table, out):
    at = pl.ds(level[0] % 8, 1)
    values = rows[...].astype(jnp.float32)
    centre = values - jnp.mean(values, -1, keepdims=True)
    spread = jnp.mean(centre * centre, -1, keepdims=True)
    out[...] = (
        centre * lax.rsqrt(spread + EPS) * (1.0 + table[1, at, :]) + table[0, at, :]
    ).astype(jnp.bfloat16)


def modulate(latents, levels, table, start, rows):
    width = latents.shape[1]
    unit = 16
    return pl.pallas_call(
        modulate_kernel,
        grid_spec=pltpu.PrefetchScalarGridSpec(
            num_scalar_prefetch=1,
            grid=(rows // unit,),
            in_specs=[
                pl.BlockSpec((unit, width), lambda i, level: (i + start // unit, 0)),
                level_spec(table),
            ],
            out_specs=pl.BlockSpec((unit, width), lambda i, level: (i, 0)),
        ),
        out_shape=jax.ShapeDtypeStruct((rows, width), jnp.bfloat16),
        compiler_params=pltpu.CompilerParams(vmem_limit_bytes=16 * MIB),
        cost_estimate=cost(10 * rows * width, 4 * rows * width + 24 * width * 4),
    )(levels, latents, table)


def project_kernel(count, *refs):
    tiles, (weight, gain, out, held, sems) = refs[:count], refs[count:]
    part = pl.program_id(0)
    first = (part == 0) & (pl.program_id(1) == 0)
    rows = tiles[0].shape[0]

    @pl.when(first)
    def _():
        copies = [
            pltpu.make_async_copy(tile, held.at[pl.ds(i * rows, rows)], sems.at[i])
            for i, tile in enumerate(tiles)
        ]
        for copy in copies:
            copy.start()
        for copy in copies:
            copy.wait()

    proj = jnp.dot(held[...], weight[0], preferred_element_type=jnp.float32)

    @pl.when(part == 2)
    def _():
        out[0] = proj.astype(jnp.bfloat16)

    @pl.when(part < 2)
    def _():
        for h in range(proj.shape[1] // HD):
            head = proj[:, h * HD : (h + 1) * HD]
            square = jnp.mean(head * head, -1, keepdims=True)
            cut = slice(h * HD, (h + 1) * HD)
            scale = jnp.where(part == 0, gain[0:1, cut], gain[1:2, cut])
            out[0, :, cut] = (
                head * lax.rsqrt(square + EPS) * scale
            ).astype(jnp.bfloat16)


def project(tiles, weight, gain):
    rows = tiles[0].shape[0] * len(tiles)
    width, cols = weight.shape[1:]
    unit = min(cols, 2 * HD)
    return pl.pallas_call(
        functools.partial(project_kernel, len(tiles)),
        grid=(3, cols // unit),
        in_specs=[pl.BlockSpec(memory_space=pl.ANY)] * len(tiles)
        + [
            pl.BlockSpec((1, width, unit), lambda p, i: (p, 0, i)),
            pl.BlockSpec((2, unit), lambda p, i: (0, i)),
        ],
        out_specs=pl.BlockSpec((1, rows, unit), lambda p, i: (p, 0, i)),
        out_shape=jax.ShapeDtypeStruct((3, rows, cols), jnp.bfloat16),
        scratch_shapes=[
            pltpu.VMEM((rows, width), jnp.bfloat16),
            pltpu.SemaphoreType.DMA((len(tiles),)),
        ],
        compiler_params=pltpu.CompilerParams(vmem_limit_bytes=32 * MIB),
        cost_estimate=cost(6 * rows * width * cols, 6 * width * cols + 2 * rows * width),
    )(*tiles, weight, gain)


def attend_kernel(pieces, behind, clip, visible, counts, *refs):
    queries = refs[:pieces]
    keys = refs[pieces : 2 * pieces]
    values = refs[2 * pieces : 3 * pieces]
    packed = refs[3 * pieces : 3 * pieces + behind]
    out = refs[-1]
    me = clip[0]
    scale = HD ** (-0.5) * LOG2E
    bias = []
    for by in range(1, behind + 1):
        source = me - by
        at = jnp.maximum(source, 0)
        limit = jnp.where((source >= 0) & (visible[me, at] == 1), counts[at], 0)
        row = lax.broadcasted_iota(jnp.int32, (1, packed[by - 1].shape[1]), 1)
        bias.append(jnp.where(row % LEAD // SPOTS < limit, 0.0, NEG))
    for h in range(out.shape[1] // HD):
        cut = slice(h * HD, (h + 1) * HD)
        key = [ref[0, :, cut] for ref in keys] + [ref[0, :, cut] for ref in packed]
        value = [ref[0, :, cut] for ref in values] + [ref[1, :, cut] for ref in packed]
        shift = [None] * pieces + bias
        begin = 0
        for query in queries:
            rows = query.shape[1]
            scores = []
            for block, add in zip(key, shift):
                score = lax.dot_general(
                    query[0, :, cut],
                    block,
                    (((1,), (1,)), ((), ())),
                    preferred_element_type=jnp.float32,
                )
                scores.append(score if add is None else score + add)
            best = functools.reduce(
                jnp.maximum, [jnp.max(score, -1, keepdims=True) for score in scores]
            )
            total = 0.0
            acc = 0.0
            for score, block in zip(scores, value):
                terms = jnp.exp2((score - best) * scale)
                total = total + jnp.sum(terms, -1, keepdims=True)
                acc = acc + jnp.dot(
                    terms.astype(jnp.bfloat16), block, preferred_element_type=jnp.float32
                )
            out[begin : begin + rows, cut] = (acc / total).astype(jnp.bfloat16)
            begin += rows


def attend(lane, parts, packed, clip, visible, counts):
    cols = parts[0].shape[2]
    own = sum(part.shape[1] for part in parts)
    seen = own + sum(block.shape[1] for block in packed)
    rows = own // CORES

    def half(part):
        return pl.BlockSpec((1, part.shape[1] // CORES, cols), lambda i: (0, lane, 0))

    def whole(part, which):
        return pl.BlockSpec((1,) + part.shape[1:], lambda i: (which, 0, 0))

    specs = [half(part) for part in parts]
    specs += [whole(part, 1) for part in parts] + [whole(part, 2) for part in parts]
    specs += [pl.BlockSpec(block.shape, lambda i: (0, 0, 0)) for block in packed]
    return pl.pallas_call(
        functools.partial(attend_kernel, len(parts), len(packed)),
        grid=(1,),
        in_specs=[smem()] * 3 + specs,
        out_specs=pl.BlockSpec((rows, cols), lambda i: (0, 0)),
        out_shape=jax.ShapeDtypeStruct((rows, cols), jnp.bfloat16),
        compiler_params=pltpu.CompilerParams(vmem_limit_bytes=32 * MIB),
        cost_estimate=cost(
            4 * rows * seen * cols, 2 * cols * (rows + 2 * seen), rows * seen * cols // HD
        ),
    )(clip, visible, counts, *parts, *parts, *parts, *packed)


def output_kernel(slots, sizes, mine, theirs, w_mine, w_theirs, *outs):
    term = jnp.dot(mine[...], w_mine[...], preferred_element_type=jnp.float32)
    term += jnp.dot(theirs[...], w_theirs[...], preferred_element_type=jnp.float32)
    term = term.astype(jnp.bfloat16)
    index = 0
    begin = 0
    for size in sizes:
        for _ in range(slots):
            outs[index][...] = term[begin : begin + size]
            begin += size
            index += 1


def output(mine, theirs, w_mine, w_theirs, slots, sizes):
    rows, cols = mine.shape
    width = w_mine.shape[1]
    unit = 512
    shapes = [size for size in sizes for _ in range(slots)]
    outs = pl.pallas_call(
        functools.partial(output_kernel, slots, sizes),
        grid=(width // unit,),
        in_specs=[pl.BlockSpec((rows, cols), lambda i: (0, 0))] * 2
        + [pl.BlockSpec((cols, unit), lambda i: (0, i))] * 2,
        out_specs=[pl.BlockSpec((size, unit), lambda i: (0, i)) for size in shapes],
        out_shape=[jax.ShapeDtypeStruct((size, width), jnp.bfloat16) for size in shapes],
        compiler_params=pltpu.CompilerParams(vmem_limit_bytes=32 * MIB),
        cost_estimate=cost(4 * rows * cols * width, 4 * cols * width + 2 * rows * width),
    )(mine, theirs, w_mine, w_theirs)
    return [outs[i * slots : (i + 1) * slots] for i in range(len(sizes))]


def residual_kernel(count, level, rows, table, head, *refs):
    terms, (denoised, feats) = refs[:count], refs[count:]
    at = pl.ds(level[0] % 8, 1)
    total = functools.reduce(lambda a, b: a + b, [term[...].astype(jnp.float32) for term in terms])
    new = (rows[...].astype(jnp.float32) + table[2, at, :] * total).astype(jnp.bfloat16)
    denoised[...] = new
    feats[...] = lax.dot_general(
        new, head[...], (((1,), (1,)), ((), ())), preferred_element_type=jnp.float32
    ).astype(jnp.bfloat16)


def residual(latents, levels, table, head, terms):
    rows, width = latents.shape
    channels = head.shape[0]
    whole = lambda i, level: (0, 0)
    return pl.pallas_call(
        functools.partial(residual_kernel, len(terms)),
        grid_spec=pltpu.PrefetchScalarGridSpec(
            num_scalar_prefetch=1,
            grid=(1,),
            in_specs=[
                pl.BlockSpec((rows, width), whole),
                level_spec(table),
                pl.BlockSpec(head.shape, whole),
            ]
            + [pl.BlockSpec((rows, width), whole)] * len(terms),
            out_specs=[
                pl.BlockSpec((rows, width), whole),
                pl.BlockSpec((rows, channels), whole),
            ],
        ),
        out_shape=[
            jax.ShapeDtypeStruct((rows, width), jnp.bfloat16),
            jax.ShapeDtypeStruct((rows, channels), jnp.bfloat16),
        ],
        compiler_params=pltpu.CompilerParams(vmem_limit_bytes=24 * MIB),
        cost_estimate=cost(
            2 * rows * width * channels, 2 * rows * width * (2 + len(terms)) + 2 * width * channels
        ),
    )(levels, latents, table, head, *terms)


def conv_kernel(earlier, feats, weight, out):
    rows = feats.shape[0]
    sequence = jnp.concatenate([earlier[...], feats[...]], 0)
    conv = jnp.zeros(out.shape, jnp.float32)
    for tap in range(3):
        begin = HALO - tap * SPOTS
        conv = conv + jnp.dot(
            sequence[begin : begin + rows], weight[tap], preferred_element_type=jnp.float32
        )
    out[...] = (conv / (1.0 + jnp.exp(-conv))).astype(jnp.bfloat16)


def conv(earlier, feats, weight):
    return pl.pallas_call(
        conv_kernel,
        in_specs=[vmem()] * 3,
        out_specs=vmem(),
        out_shape=jax.ShapeDtypeStruct((feats.shape[0], weight.shape[2]), jnp.bfloat16),
        compiler_params=pltpu.CompilerParams(vmem_limit_bytes=16 * MIB),
        cost_estimate=cost(6 * feats.shape[0] * weight.shape[1] * weight.shape[2], 400000),
    )(earlier, feats, weight)


def spread(tile, table, place):
    held = []
    for entries in table:
        got = None
        for pairs, source in entries:
            came = lax.ppermute(tile if source is None else held[source], "tok", lanes(pairs))
            if got is None:
                got = came
            else:
                takes = functools.reduce(lambda a, b: a | b, [place == b for _, b in pairs])
                got = jnp.where(takes, came, got)
        held.append(got)
    return [tile] + held


def gather_sums(terms, table):
    own, sent = terms[0], list(terms[1:])
    arrived = []
    for slot in reversed(range(len(table))):
        for pairs, source in table[slot]:
            came = lax.ppermute(sent[slot], "tok", lanes(back(pairs)))
            if source is None:
                arrived.append(came)
            else:
                sent[source] = (
                    sent[source].astype(jnp.float32) + came.astype(jnp.float32)
                ).astype(jnp.bfloat16)
    return [own] + arrived


def per_device(
    latents, levels, visible, frame_counts, modulation, w_qkv, qk_gain, w_out, w_head, conv_w
):
    current = latents[0]
    line = lax.axis_size("tok") // CORES
    place = lax.axis_index("tok") // CORES
    clip = lax.axis_index("span").astype(jnp.int32).reshape(1)
    table = routes(line)
    slots = line
    mods = modulation.transpose(1, 0, 2)
    weight = w_qkv.transpose(1, 0, 2)
    head = w_head.transpose(1, 0)
    w_theirs = over_core(w_out)

    modulated = modulate(current, levels, mods, 0, TOK_DEV)
    lane = spread(modulated, table, place)
    tiles = lane + [over_core(tile) for tile in lane]
    qkv = project(tiles, weight, qk_gain)

    cols = qkv.shape[2]
    lead = qkv.reshape(3, len(tiles), TOK_DEV, cols)[1:, :, :LEAD].reshape(2, -1, cols)
    packed = [from_behind(lead, "span", by) for by in range(1, lax.axis_size("span"))]

    theirs = attend(1, [qkv], packed, clip, visible, frame_counts)
    theirs = over_core(theirs)
    mine = attend(0, [qkv], packed, clip, visible, frame_counts)
    terms = output(mine, theirs, w_out, w_theirs, slots, [TOK_DEV])[0]
    sums = gather_sums(terms, table)
    denoised, feats = residual(current, levels, mods, head, sums)
    earlier = from_behind(feats[TOK_DEV - HALO :], "span", 1)
    decoded = conv(earlier, feats, conv_w)
    return (denoised[None], decoded[None])


def solution(mesh):
    placed = (
        P("span", "tok", None),
        P("span"),
        P(),
        P(),
        P(),
        P(None, None, "tok"),
        P(None, "tok"),
        P("tok", None),
        P(),
        P(),
    )
    return jax.shard_map(
        per_device,
        mesh=mesh,
        in_specs=placed,
        out_specs=(P("span", "tok", None), P("span", "tok", None)),
        check_vma=False,
    )
```

```python
import functools

import jax
import jax.numpy as jnp
from jax import lax
from jax.experimental import pallas as pl
from jax.experimental.pallas import tpu as pltpu
from jax.sharding import PartitionSpec as P

HD = 128
FRAMES = 8
KEEP = 2
SPOTS = 8
TOK_DEV = 64
CORES = 2
LEAD = KEEP * SPOTS
HALO = 2 * SPOTS
BODY = TOK_DEV - LEAD
END = 32
REST = TOK_DEV - END


EPS = 1e-06
NEG = -1e30
LOG2E = 1.4426950408889634
MIB = 1 << 20


def routes(line):
    if line == 4:
        return [
            ([(0, 2), (2, 3), (3, 1), (1, 0)], None),
            ([(0, 1), (1, 3), (3, 2), (2, 0)], None),
            ([(0, 1), (1, 0), (2, 3), (3, 2)], (1, 0, 0, 1)),
        ]
    return [([(i, (i + by) % line) for i in range(line)], None) for by in range(1, line)]


def direct(table):
    def origin(place, relay):
        if relay is None:
            return place
        return next(a for a, b in table[relay[place]][0] if b == place)

    return [([(origin(a, relay), b) for a, b in pairs], None) for pairs, relay in table]


def lanes(pairs):
    return [(a * CORES + c, b * CORES + c) for a, b in pairs for c in range(CORES)]


def back(pairs):
    return [(b, a) for a, b in pairs]


def after(array, *others):
    return lax.optimization_barrier((array,) + others)[0]


def over_core(array):
    devices = lax.axis_size("tok")
    return lax.ppermute(array, "tok", [(i, i ^ 1) for i in range(devices)])


def from_behind(array, axis, by):
    devices = lax.axis_size(axis)
    pairs = [(i, i + by) for i in range(devices) if 0 <= i + by < devices]
    return lax.ppermute(array, axis, pairs)


def from_earlier(array):
    devices = lax.axis_size("span")
    if devices != 4:
        steps = range(1, devices)
        came = [from_behind(array, "span", by) for by in steps]
        return came, [lambda me, by=by: me - by for by in steps]
    beside = lax.ppermute(array, "span", [(0, 1), (2, 3)])
    behind = lax.ppermute(array, "span", [(0, 2), (1, 3)])
    across = lax.ppermute(after(behind, beside), "span", [(3, 2), (2, 3)])
    return [beside, behind, across], [
        lambda me: jnp.where(me % 2 == 1, me - 1, -1),
        lambda me: me - 2,
        lambda me: jnp.where(me % 2 == 1, me - 3, me - 1),
    ]


def vmem():
    return pl.BlockSpec(memory_space=pltpu.VMEM)


def smem():
    return pl.BlockSpec(memory_space=pltpu.SMEM)


def hbm():
    return pl.BlockSpec(memory_space=pltpu.HBM)


def in_hbm(array):
    return pltpu.with_memory_space_constraint(array, pltpu.HBM)


def in_vmem(array):
    return pltpu.with_memory_space_constraint(array, pltpu.VMEM)


CHEAP = pl.CostEstimate(flops=1, bytes_accessed=1, transcendentals=0)


def params(mib):
    return pltpu.CompilerParams(vmem_limit_bytes=mib * MIB)


def modulate_kernel(level, rows, table, lead, body, held, mods, sems):
    base = pl.multiple_of(level[0] // 8 * 8, 8)
    copies = [
        pltpu.make_async_copy(rows, held, sems.at[0]),
        pltpu.make_async_copy(table.at[pl.ds(0, 2), pl.ds(base, 8)], mods, sems.at[1]),
    ]
    for copy in copies:
        copy.start()
    for copy in copies:
        copy.wait()
    at = pl.ds(level[0] % 8, 1)
    begin = 0
    for out in (lead, body):
        values = held[begin : begin + out.shape[0]].astype(jnp.float32)
        centre = values - jnp.mean(values, -1, keepdims=True)
        spread = jnp.mean(centre * centre, -1, keepdims=True)
        out[...] = (
            centre * lax.rsqrt(spread + EPS) * (1.0 + mods[1, at, :]) + mods[0, at, :]
        ).astype(jnp.bfloat16)
        begin += out.shape[0]


def modulate(latents, levels, table):
    rows, width = latents.shape
    return pl.pallas_call(
        modulate_kernel,
        in_specs=[smem(), hbm(), hbm()],
        out_specs=[vmem()] * 2,
        out_shape=[
            jax.ShapeDtypeStruct((part, width), jnp.bfloat16) for part in (LEAD, rows - LEAD)
        ],
        scratch_shapes=[
            pltpu.VMEM((rows, width), jnp.bfloat16),
            pltpu.VMEM((2, 8, width), jnp.float32),
            pltpu.SemaphoreType.DMA((2,)),
        ],
        compiler_params=params(8),
        cost_estimate=CHEAP,
    )(levels, in_hbm(latents), in_hbm(table))


def project_kernel(count, *refs):
    tiles, (gain, weight, out, kept, held, sems) = refs[:count], refs[count:]
    cols = weight.shape[2]
    unit = cols
    blocks = [(part, begin) for part in range(3) for begin in range(0, cols, unit)]
    copies = [
        pltpu.make_async_copy(
            weight.at[part, :, pl.ds(begin, unit)],
            kept.at[part, :, pl.ds(begin, unit)],
            sems.at[i],
        )
        for i, (part, begin) in enumerate(blocks)
    ]
    for copy in copies:
        copy.start()
    begin = 0
    for tile in tiles:
        held[begin : begin + tile.shape[0]] = tile[...]
        begin += tile.shape[0]
    for copy, (part, begin) in zip(copies, blocks):
        copy.wait()
        proj = jnp.dot(
            held[...], kept[part, :, begin : begin + unit], preferred_element_type=jnp.float32
        )
        if part == 2:
            out[part, :, begin : begin + unit] = proj.astype(jnp.bfloat16)
            continue
        for h in range(unit // HD):
            cut = slice(begin + h * HD, begin + (h + 1) * HD)
            head = proj[:, h * HD : (h + 1) * HD]
            square = jnp.mean(head * head, -1, keepdims=True)
            out[part, :, cut] = (
                head * lax.rsqrt(square + EPS) * gain[part : part + 1, cut]
            ).astype(jnp.bfloat16)


def project(tiles, gain, weight):
    rows = sum(tile.shape[0] for tile in tiles)
    width, cols = weight.shape[1:]
    return pl.pallas_call(
        functools.partial(project_kernel, len(tiles)),
        in_specs=[vmem()] * (len(tiles) + 1) + [hbm()],
        out_specs=vmem(),
        out_shape=jax.ShapeDtypeStruct((3, rows, cols), jnp.bfloat16),
        scratch_shapes=[
            pltpu.VMEM(weight.shape, weight.dtype),
            pltpu.VMEM((rows, width), jnp.bfloat16),
            pltpu.SemaphoreType.DMA((3,)),
        ],
        compiler_params=params(18 + rows // 64 // 8),
        cost_estimate=CHEAP,
    )(*tiles, gain, in_hbm(weight))


def attend_kernel(cuts, own, origins, clip, visible, counts, *refs):
    parts = refs[:own]
    behind = len(origins)
    packed = refs[own : own + behind]
    weight, out, kept, sem = refs[own + behind :]
    copy = pltpu.make_async_copy(weight, kept, sem)
    copy.start()
    me = clip[0]
    scale = HD ** (-0.5) * LOG2E
    bias = []
    for origin, block in zip(origins, packed):
        source = origin(me)
        at = jnp.maximum(source, 0)
        limit = jnp.where((source >= 0) & (visible[me, at] == 1), counts[at], 0)
        row = lax.broadcasted_iota(jnp.int32, (1, block.shape[1]), 1)
        bias.append(jnp.where(row % LEAD // SPOTS < limit, 0.0, NEG))
    heads = [slice(h * HD, (h + 1) * HD) for h in range(out.shape[1] // HD)]
    scores = []
    for cut in heads:
        query = jnp.concatenate(
            [parts[part][0, begin:end, cut] for part, begin, end in cuts], 0
        )
        keys = [(ref[1, :, cut], None) for ref in parts]
        keys += [(ref[0, :, cut], add) for ref, add in zip(packed, bias)]
        row = []
        for key, add in keys:
            score = lax.dot_general(
                query, key, (((1,), (1,)), ((), ())), preferred_element_type=jnp.float32
            )
            row.append(score if add is None else score + add)
        scores.append(row)
    terms, totals = [], []
    for row in scores:
        best = functools.reduce(jnp.maximum, [jnp.max(score, -1, keepdims=True) for score in row])
        row = [jnp.exp2((score - best) * scale) for score in row]
        totals.append(sum(jnp.sum(term, -1, keepdims=True) for term in row))
        terms.append([term.astype(jnp.bfloat16) for term in row])
    for cut, row, total in zip(heads, terms, totals):
        values = [ref[2, :, cut] for ref in parts]
        values += [ref[1, :, cut] for ref in packed]
        acc = sum(
            jnp.dot(term, value, preferred_element_type=jnp.float32)
            for term, value in zip(row, values)
        )
        out[:, cut] = (acc / total).astype(jnp.bfloat16)
    copy.wait()


def attend(cuts, parts, packed, origins, clip, visible, counts, weight):
    cols = parts[0].shape[2]
    seen = sum(part.shape[1] for part in parts)
    seen += sum(block.shape[1] for block in packed)
    rows = sum(end - begin for _, begin, end in cuts)
    return pl.pallas_call(
        functools.partial(attend_kernel, cuts, len(parts), origins),
        in_specs=[smem()] * 3 + [vmem()] * (len(parts) + len(packed)) + [hbm()],
        out_specs=[vmem()] * 2,
        out_shape=[
            jax.ShapeDtypeStruct((rows, cols), jnp.bfloat16),
            pltpu.VMEM(weight.shape, weight.dtype),
        ],
        scratch_shapes=[pltpu.SemaphoreType.DMA],
        compiler_params=params(max(10, 12 * rows * seen * cols // HD // MIB)),
        cost_estimate=CHEAP,
    )(clip, visible, counts, *parts, *packed, in_hbm(weight))


def output_kernel(attended, weight, *outs):
    unit = 512
    for column in range(0, weight.shape[1], unit):
        cut = slice(column, column + unit)
        term = jnp.dot(attended[...], weight[:, cut], preferred_element_type=jnp.float32)
        term = term.astype(jnp.bfloat16)
        begin = 0
        for out in outs:
            out[:, cut] = term[begin : begin + out.shape[0]]
            begin += out.shape[0]


def output(attended, weight, slots):
    rows, cols = attended.shape
    width = weight.shape[1]
    unit = rows // (CORES * slots)
    sizes = [unit] * slots + [unit * (slots - 1), unit]
    return pl.pallas_call(
        output_kernel,
        in_specs=[vmem()] * 2,
        out_specs=[vmem()] * len(sizes),
        out_shape=[jax.ShapeDtypeStruct((size, width), jnp.bfloat16) for size in sizes],
        compiler_params=params(10),
        cost_estimate=CHEAP,
    )(attended, in_vmem(weight))


def fold(rows, gate, terms):
    total = functools.reduce(lambda a, b: a + b, [term[...].astype(jnp.float32) for term in terms])
    return (rows.astype(jnp.float32) + gate * total).astype(jnp.bfloat16)


def project_head(rows, head):
    return lax.dot_general(
        rows, head, (((1,), (1,)), ((), ())), preferred_element_type=jnp.float32
    ).astype(jnp.bfloat16)


def end_kernel(level, rows, table, head, *refs):
    terms, (new, feats) = refs[:-2], refs[-2:]
    gate = table[2, pl.ds(level[0], 1), :]
    new[...] = fold(rows[REST:, :], gate, terms)
    feats[...] = project_head(new[...], head[...])


def end_rows(latents, levels, table, head, terms):
    rows, width = terms[0].shape
    channels = head.shape[0]
    return pl.pallas_call(
        end_kernel,
        in_specs=[smem()] + [vmem()] * (3 + len(terms)),
        out_specs=[vmem()] * 2,
        out_shape=[
            jax.ShapeDtypeStruct((rows, width), jnp.bfloat16),
            jax.ShapeDtypeStruct((rows, channels), jnp.bfloat16),
        ],
        compiler_params=params(8),
        cost_estimate=CHEAP,
    )(levels, latents, table, head, *terms)


def finish_kernel(level, rows, table, head, weight, earlier, end, end_feats, *refs):
    terms, (denoised, decoded) = refs[:-2], refs[-2:]
    gate = table[2, pl.ds(level[0], 1), :]
    new = fold(rows[:REST, :], gate, terms)
    denoised[:REST] = new
    denoised[REST:] = end[...]
    feats = project_head(new, head[...])
    sequence = jnp.concatenate([earlier[...], feats, end_feats[...]], 0)
    conv = jnp.zeros(decoded.shape, jnp.float32)
    for tap in range(3):
        begin = HALO - tap * SPOTS
        conv = conv + jnp.dot(
            sequence[begin : begin + TOK_DEV], weight[tap], preferred_element_type=jnp.float32
        )
    decoded[...] = (conv / (1.0 + jnp.exp(-conv))).astype(jnp.bfloat16)


def finish(latents, levels, table, head, weight, earlier, end, end_feats, terms):
    rows, width = latents.shape
    return pl.pallas_call(
        finish_kernel,
        in_specs=[smem()] + [vmem()] * (7 + len(terms)),
        out_specs=[vmem()] * 2,
        out_shape=[
            jax.ShapeDtypeStruct((rows, width), jnp.bfloat16),
            jax.ShapeDtypeStruct((rows, weight.shape[2]), jnp.bfloat16),
        ],
        compiler_params=params(8),
        cost_estimate=CHEAP,
    )(levels, latents, table, head, weight, earlier, end, end_feats, *terms)


def passes(relay, slot, place):
    return functools.reduce(
        lambda a, b: a | b, [place == at for at, kept in enumerate(relay) if kept == slot]
    )


def take(entry, tile, held, place):
    pairs, relay = entry
    if relay is not None:
        first, *others = sorted(set(relay))
        tile = held[first]
        for slot in others:
            tile = jnp.where(passes(relay, slot, place), held[slot], tile)
    return lax.ppermute(tile, "tok", lanes(pairs))


def spread(tile, table, place):
    held = []
    for entry in table:
        held.append(take(entry, tile, held, place))
    return held


def total(*terms):
    return functools.reduce(
        lambda a, b: a + b, [term.astype(jnp.float32) for term in terms]
    ).astype(jnp.bfloat16)


def passed_back(attended, weight, table, place, *wait):
    slots = len(table) + 1
    *mine, others, last = output(attended, weight, slots)
    last = over_core(after(last, *wait))
    others = jnp.split(over_core(others), slots - 1, 0)
    sent = [[a, b] for a, b in zip(mine[1:], others[1:] + [last])]
    for slot in reversed(range(len(table))):
        pairs, relay = table[slot]
        if relay is None:
            continue
        came = lax.ppermute(total(*sent[slot]), "tok", lanes(back(pairs)))
        for kept in set(relay):
            sent[kept].append(jnp.where(passes(relay, kept, place), came, jnp.bfloat16(0.0)))
    sent = [total(*terms) for terms, (_, relay) in zip(sent, table) if relay is None]
    return [mine[0], others[0]], sent


def sent_home(sent, table):
    direct = [pairs for pairs, relay in table if relay is None]
    return [
        lax.ppermute(term, "tok", lanes(back(pairs))) for term, pairs in zip(sent, direct)
    ]


def per_device(
    latents, levels, visible, frame_counts, modulation, w_qkv, qk_gain, w_out, w_head, conv_w
):
    current = latents[0]
    line = lax.axis_size("tok") // CORES
    place = lax.axis_index("tok") // CORES
    clip = lax.axis_index("span").astype(jnp.int32).reshape(1)
    table = routes(line)
    mods = modulation.transpose(1, 0, 2)
    weight = w_qkv.transpose(1, 0, 2)
    head = w_head.transpose(1, 0)

    lead, body = modulate(current, levels, mods)
    leads = [lead] + spread(lead, direct(table), place)
    held = spread(body, table[:-1], place)
    half = line // 2
    for part in (leads[:half], leads[half:]):
        pair = over_core(jnp.concatenate(part, 0))
        leads = leads + jnp.split(pair, half, 0)
    lead_part = project(leads, qk_gain, weight)
    packed, origins = from_earlier(lead_part[1:])

    last = take(table[-1], body, [after(tile, lead_part) for tile in held], place)
    across = over_core(jnp.concatenate([body] + held, 0))
    early_part = project([body] + held + [across], qk_gain, weight)
    last = after(last, early_part)
    late_part = project([last, over_core(last)], qk_gain, weight)
    parts = [lead_part, early_part, late_part]

    def at(lane, slot):
        if slot < line - 1:
            return 1, (lane * (line - 1) + slot) * BODY
        return 2, lane * BODY

    def attended(tail, parts):
        cuts = []
        for lane in range(CORES):
            for slot in range(line):
                part, begin = at(lane, slot)
                middle = begin + BODY - END
                if tail:
                    cuts.append((part, middle, middle + END))
                else:
                    begin_lead = (lane * line + slot) * LEAD
                    cuts.append((0, begin_lead, begin_lead + LEAD))
                    cuts.append((part, begin, middle))
        return attend(cuts, parts, packed, origins, clip, visible, frame_counts, w_out)

    own_end, end_sent = passed_back(*attended(True, parts), table, place)
    parts[-1] = after(parts[-1], own_end[0])
    own, sent = passed_back(*attended(False, parts), table, place, *end_sent)

    end_sums = own_end + sent_home(end_sent, table)
    end, end_feats = end_rows(current, levels, mods, head, end_sums)
    earlier = from_behind(end_feats[END - HALO :], "span", 1)
    sums = own + sent_home([after(term, end_feats) for term in sent], table)
    denoised, decoded = finish(
        current, levels, mods, head, conv_w, earlier, end, end_feats, sums
    )
    return (denoised[None], decoded[None])


def solution(mesh):
    placed = (
        P("span", "tok", None),
        P("span"),
        P(),
        P(),
        P(),
        P(None, None, "tok"),
        P(None, "tok"),
        P("tok", None),
        P(),
        P(),
    )
    return jax.shard_map(
        per_device,
        mesh=mesh,
        in_specs=placed,
        out_specs=(P("span", "tok", None), P("span", "tok", None)),
        check_vma=False,
    )
```

```python
import functools

import jax
import jax.numpy as jnp
from jax import lax
from jax.experimental import pallas as pl
from jax.experimental.pallas import tpu as pltpu
from jax.sharding import PartitionSpec as P

HD = 128
FRAMES = 8
KEEP = 2
SPOTS = 8
TOK_DEV = 64
CORES = 2
LEAD = KEEP * SPOTS
HALO = 2 * SPOTS
BODY = TOK_DEV - LEAD
END = 32
REST = TOK_DEV - END


EPS = 1e-06
NEG = -1e30
LOG2E = 1.4426950408889634
MIB = 1 << 20


def routes(line):
    if line == 4:
        return [
            ([(0, 2), (2, 3), (3, 1), (1, 0)], None),
            ([(0, 1), (1, 3), (3, 2), (2, 0)], None),
            ([(0, 1), (1, 0), (2, 3), (3, 2)], (1, 0, 0, 1)),
        ]
    return [([(i, (i + by) % line) for i in range(line)], None) for by in range(1, line)]


def direct(table):
    def origin(place, relay):
        if relay is None:
            return place
        return next(a for a, b in table[relay[place]][0] if b == place)

    return [([(origin(a, relay), b) for a, b in pairs], None) for pairs, relay in table]


def lanes(pairs):
    return [(a * CORES + c, b * CORES + c) for a, b in pairs for c in range(CORES)]


def back(pairs):
    return [(b, a) for a, b in pairs]


def after(array, *others):
    return lax.optimization_barrier((array,) + others)[0]


def over_core(array):
    devices = lax.axis_size("tok")
    return lax.ppermute(array, "tok", [(i, i ^ 1) for i in range(devices)])


def from_behind(array, axis, by):
    devices = lax.axis_size(axis)
    pairs = [(i, i + by) for i in range(devices) if 0 <= i + by < devices]
    return lax.ppermute(array, axis, pairs)


def from_earlier(array):
    devices = lax.axis_size("span")
    if devices != 4:
        steps = range(1, devices)
        came = [from_behind(array, "span", by) for by in steps]
        return came, [lambda me, by=by: me - by for by in steps]
    beside = lax.ppermute(array, "span", [(0, 1), (2, 3)])
    behind = lax.ppermute(array, "span", [(0, 2), (1, 3)])
    across = lax.ppermute(after(behind, beside), "span", [(3, 2), (2, 3)])
    return [beside, behind, across], [
        lambda me: jnp.where(me % 2 == 1, me - 1, -1),
        lambda me: me - 2,
        lambda me: jnp.where(me % 2 == 1, me - 3, me - 1),
    ]


def vmem():
    return pl.BlockSpec(memory_space=pltpu.VMEM)


def smem():
    return pl.BlockSpec(memory_space=pltpu.SMEM)


def hbm():
    return pl.BlockSpec(memory_space=pltpu.HBM)


def in_hbm(array):
    return pltpu.with_memory_space_constraint(array, pltpu.HBM)


def in_vmem(array):
    return pltpu.with_memory_space_constraint(array, pltpu.VMEM)


CHEAP = pl.CostEstimate(flops=1, bytes_accessed=1, transcendentals=0)


def params(mib):
    return pltpu.CompilerParams(vmem_limit_bytes=mib * MIB)


def modulate_kernel(level, rows, table, lead, body, held, mods, sems):
    base = pl.multiple_of(level[0] // 8 * 8, 8)
    copies = [
        pltpu.make_async_copy(rows, held, sems.at[0]),
        pltpu.make_async_copy(table.at[pl.ds(0, 2), pl.ds(base, 8)], mods, sems.at[1]),
    ]
    for copy in copies:
        copy.start()
    for copy in copies:
        copy.wait()
    at = pl.ds(level[0] % 8, 1)
    begin = 0
    for out in (lead, body):
        values = held[begin : begin + out.shape[0]].astype(jnp.float32)
        centre = values - jnp.mean(values, -1, keepdims=True)
        spread = jnp.mean(centre * centre, -1, keepdims=True)
        out[...] = (
            centre * lax.rsqrt(spread + EPS) * (1.0 + mods[1, at, :]) + mods[0, at, :]
        ).astype(jnp.bfloat16)
        begin += out.shape[0]


def modulate(latents, levels, table):
    rows, width = latents.shape
    return pl.pallas_call(
        modulate_kernel,
        in_specs=[smem(), hbm(), hbm()],
        out_specs=[vmem()] * 2,
        out_shape=[
            jax.ShapeDtypeStruct((part, width), jnp.bfloat16) for part in (LEAD, rows - LEAD)
        ],
        scratch_shapes=[
            pltpu.VMEM((rows, width), jnp.bfloat16),
            pltpu.VMEM((2, 8, width), jnp.float32),
            pltpu.SemaphoreType.DMA((2,)),
        ],
        compiler_params=params(8),
        cost_estimate=CHEAP,
    )(levels, in_hbm(latents), in_hbm(table))


def project_kernel(count, *refs):
    tiles, (gain, weight, out, kept, held, sems) = refs[:count], refs[count:]
    cols = weight.shape[2]
    unit = cols
    blocks = [(part, begin) for part in range(3) for begin in range(0, cols, unit)]
    copies = [
        pltpu.make_async_copy(
            weight.at[part, :, pl.ds(begin, unit)],
            kept.at[part, :, pl.ds(begin, unit)],
            sems.at[i],
        )
        for i, (part, begin) in enumerate(blocks)
    ]
    for copy in copies:
        copy.start()
    begin = 0
    for tile in tiles:
        held[begin : begin + tile.shape[0]] = tile[...]
        begin += tile.shape[0]
    for copy, (part, begin) in zip(copies, blocks):
        copy.wait()
        proj = jnp.dot(
            held[...], kept[part, :, begin : begin + unit], preferred_element_type=jnp.float32
        )
        if part == 2:
            out[part, :, begin : begin + unit] = proj.astype(jnp.bfloat16)
            continue
        for h in range(unit // HD):
            cut = slice(begin + h * HD, begin + (h + 1) * HD)
            head = proj[:, h * HD : (h + 1) * HD]
            square = jnp.mean(head * head, -1, keepdims=True)
            out[part, :, cut] = (
                head * lax.rsqrt(square + EPS) * gain[part : part + 1, cut]
            ).astype(jnp.bfloat16)


def project(tiles, gain, weight):
    rows = sum(tile.shape[0] for tile in tiles)
    width, cols = weight.shape[1:]
    return pl.pallas_call(
        functools.partial(project_kernel, len(tiles)),
        in_specs=[vmem()] * (len(tiles) + 1) + [hbm()],
        out_specs=vmem(),
        out_shape=jax.ShapeDtypeStruct((3, rows, cols), jnp.bfloat16),
        scratch_shapes=[
            pltpu.VMEM(weight.shape, weight.dtype),
            pltpu.VMEM((rows, width), jnp.bfloat16),
            pltpu.SemaphoreType.DMA((3,)),
        ],
        compiler_params=params(18 + rows // 64 // 8),
        cost_estimate=CHEAP,
    )(*tiles, gain, in_hbm(weight))


def attend_kernel(cuts, own, origins, clip, visible, counts, *refs):
    parts = refs[:own]
    behind = len(origins)
    packed = refs[own : own + behind]
    weight, out, kept, sem = refs[own + behind :]
    copy = pltpu.make_async_copy(weight, kept, sem)
    copy.start()
    me = clip[0]
    scale = HD ** (-0.5) * LOG2E
    bias = []
    for origin, block in zip(origins, packed):
        source = origin(me)
        at = jnp.maximum(source, 0)
        limit = jnp.where((source >= 0) & (visible[me, at] == 1), counts[at], 0)
        row = lax.broadcasted_iota(jnp.int32, (1, block.shape[1]), 1)
        bias.append(jnp.where(row % LEAD // SPOTS < limit, 0.0, NEG))
    heads = [slice(h * HD, (h + 1) * HD) for h in range(out.shape[1] // HD)]
    scores = []
    for cut in heads:
        query = jnp.concatenate(
            [parts[part][0, begin:end, cut] for part, begin, end in cuts], 0
        )
        keys = [(ref[1, :, cut], None) for ref in parts]
        keys += [(ref[0, :, cut], add) for ref, add in zip(packed, bias)]
        row = []
        for key, add in keys:
            score = lax.dot_general(
                query, key, (((1,), (1,)), ((), ())), preferred_element_type=jnp.float32
            )
            row.append(score if add is None else score + add)
        scores.append(row)
    terms, totals = [], []
    for row in scores:
        best = functools.reduce(jnp.maximum, [jnp.max(score, -1, keepdims=True) for score in row])
        row = [jnp.exp2((score - best) * scale) for score in row]
        totals.append(sum(jnp.sum(term, -1, keepdims=True) for term in row))
        terms.append([term.astype(jnp.bfloat16) for term in row])
    for cut, row, total in zip(heads, terms, totals):
        values = [ref[2, :, cut] for ref in parts]
        values += [ref[1, :, cut] for ref in packed]
        acc = sum(
            jnp.dot(term, value, preferred_element_type=jnp.float32)
            for term, value in zip(row, values)
        )
        out[:, cut] = (acc / total).astype(jnp.bfloat16)
    copy.wait()


def attend(cuts, parts, packed, origins, clip, visible, counts, weight):
    cols = parts[0].shape[2]
    seen = sum(part.shape[1] for part in parts)
    seen += sum(block.shape[1] for block in packed)
    rows = sum(end - begin for _, begin, end in cuts)
    return pl.pallas_call(
        functools.partial(attend_kernel, cuts, len(parts), origins),
        in_specs=[smem()] * 3 + [vmem()] * (len(parts) + len(packed)) + [hbm()],
        out_specs=[vmem()] * 2,
        out_shape=[
            jax.ShapeDtypeStruct((rows, cols), jnp.bfloat16),
            pltpu.VMEM(weight.shape, weight.dtype),
        ],
        scratch_shapes=[pltpu.SemaphoreType.DMA],
        compiler_params=params(max(10, 12 * rows * seen * cols // HD // MIB)),
        cost_estimate=CHEAP,
    )(clip, visible, counts, *parts, *packed, in_hbm(weight))


def output_kernel(attended, weight, *outs):
    unit = 512
    for column in range(0, weight.shape[1], unit):
        cut = slice(column, column + unit)
        term = jnp.dot(attended[...], weight[:, cut], preferred_element_type=jnp.float32)
        term = term.astype(jnp.bfloat16)
        begin = 0
        for out in outs:
            out[:, cut] = term[begin : begin + out.shape[0]]
            begin += out.shape[0]


def output(attended, weight, slots):
    rows, cols = attended.shape
    width = weight.shape[1]
    unit = rows // (CORES * slots)
    sizes = [unit] * slots + [unit * (slots - 1), unit]
    return pl.pallas_call(
        output_kernel,
        in_specs=[vmem()] * 2,
        out_specs=[vmem()] * len(sizes),
        out_shape=[jax.ShapeDtypeStruct((size, width), jnp.bfloat16) for size in sizes],
        compiler_params=params(10),
        cost_estimate=CHEAP,
    )(attended, in_vmem(weight))


def fold(rows, gate, terms):
    size = rows.shape[0]
    total = functools.reduce(lambda a, b: a + b, [term[:size].astype(jnp.float32) for term in terms])
    return (rows.astype(jnp.float32) + gate * total).astype(jnp.bfloat16)


def project_head(rows, head):
    return lax.dot_general(
        rows, head, (((1,), (1,)), ((), ())), preferred_element_type=jnp.float32
    ).astype(jnp.bfloat16)


def end_kernel(level, rows, table, head, *refs):
    terms, (new, feats) = refs[:-2], refs[-2:]
    gate = table[2, pl.ds(level[0], 1), :]
    new[...] = fold(rows[REST:, :], gate, terms)
    feats[...] = project_head(new[...], head[...])


def end_rows(latents, levels, table, head, terms):
    rows, width = terms[0].shape
    channels = head.shape[0]
    return pl.pallas_call(
        end_kernel,
        in_specs=[smem()] + [vmem()] * (3 + len(terms)),
        out_specs=[vmem()] * 2,
        out_shape=[
            jax.ShapeDtypeStruct((rows, width), jnp.bfloat16),
            jax.ShapeDtypeStruct((rows, channels), jnp.bfloat16),
        ],
        compiler_params=params(8),
        cost_estimate=CHEAP,
    )(levels, latents, table, head, *terms)


def finish_kernel(level, rows, table, head, weight, earlier, end, end_feats, *refs):
    terms, (denoised, decoded) = refs[:-2], refs[-2:]
    gate = table[2, pl.ds(level[0], 1), :]
    new = fold(rows[:REST, :], gate, terms)
    denoised[:REST] = new
    denoised[REST:] = end[...]
    feats = project_head(new, head[...])
    sequence = jnp.concatenate([earlier[...], feats, end_feats[...]], 0)
    conv = jnp.zeros(decoded.shape, jnp.float32)
    for tap in range(3):
        begin = HALO - tap * SPOTS
        conv = conv + jnp.dot(
            sequence[begin : begin + TOK_DEV], weight[tap], preferred_element_type=jnp.float32
        )
    decoded[...] = (conv / (1.0 + jnp.exp(-conv))).astype(jnp.bfloat16)


def finish(latents, levels, table, head, weight, earlier, end, end_feats, terms):
    rows, width = latents.shape
    return pl.pallas_call(
        finish_kernel,
        in_specs=[smem()] + [vmem()] * (7 + len(terms)),
        out_specs=[vmem()] * 2,
        out_shape=[
            jax.ShapeDtypeStruct((rows, width), jnp.bfloat16),
            jax.ShapeDtypeStruct((rows, weight.shape[2]), jnp.bfloat16),
        ],
        compiler_params=params(8),
        cost_estimate=CHEAP,
    )(levels, latents, table, head, weight, earlier, end, end_feats, *terms)


def passes(relay, slot, place):
    return functools.reduce(
        lambda a, b: a | b, [place == at for at, kept in enumerate(relay) if kept == slot]
    )


def take(entry, tile, held, place):
    pairs, relay = entry
    if relay is not None:
        first, *others = sorted(set(relay))
        tile = held[first]
        for slot in others:
            tile = jnp.where(passes(relay, slot, place), held[slot], tile)
    return lax.ppermute(tile, "tok", lanes(pairs))


def spread(tile, table, place):
    held = []
    for entry in table:
        held.append(take(entry, tile, held, place))
    return held


def merge_kernel(groups, count, place, *refs):
    arrays, outs = refs[:count], refs[count:]
    for out, group in zip(outs, groups):
        rows = out.shape[0]
        sums = 0.0
        for which, block, places in group:
            term = arrays[which][block * rows : (block + 1) * rows].astype(jnp.float32)
            if places is not None:
                here = functools.reduce(lambda a, b: a | b, [place[0] == p for p in places])
                term = jnp.where(here, term, 0.0)
            sums = sums + term
        out[...] = sums.astype(jnp.bfloat16)


def merge(place, arrays, groups):
    unit = arrays[0].shape
    return pl.pallas_call(
        functools.partial(merge_kernel, groups, len(arrays)),
        in_specs=[smem()] + [vmem()] * len(arrays),
        out_specs=[vmem()] * len(groups),
        out_shape=[jax.ShapeDtypeStruct(unit, jnp.bfloat16)] * len(groups),
        compiler_params=params(8),
        cost_estimate=CHEAP,
    )(place, *arrays)


def passed_back(terms, table, place):
    *mine, others, last = terms
    last = over_core(last)
    others = over_core(others)
    final = len(table) - 1
    passed = []
    for slot, (pairs, relay) in enumerate(table):
        if relay is not None:
            theirs = (last, 0) if slot == final else (others, slot + 1)
            (sums,) = merge(place, [mine[slot + 1], theirs[0]], [[(0, 0, None), (1, theirs[1], None)]])
            came = lax.ppermute(sums, "tok", lanes(back(pairs)))
            passed.append((came, relay))
    arrays = mine[1:] + [others, last] + [came for came, _ in passed]
    groups = []
    for slot, (_, relay) in enumerate(table):
        if relay is not None:
            continue
        group = [(slot, 0, None)]
        group.append((final + 2, 0, None) if slot == final else (final + 1, slot + 1, None))
        for i, (_, kept) in enumerate(passed):
            places = [at for at, which in enumerate(kept) if which == slot]
            group.append((final + 3 + i, 0, places))
        groups.append(group)
    return [mine[0], others], merge(place, arrays, groups)


def sent_home(sent, table):
    direct = [pairs for pairs, relay in table if relay is None]
    return [
        lax.ppermute(term, "tok", lanes(back(pairs))) for term, pairs in zip(sent, direct)
    ]


def per_device(
    latents, levels, visible, frame_counts, modulation, w_qkv, qk_gain, w_out, w_head, conv_w
):
    current = latents[0]
    line = lax.axis_size("tok") // CORES
    place = lax.axis_index("tok") // CORES
    clip = lax.axis_index("span").astype(jnp.int32).reshape(1)
    table = routes(line)
    mods = modulation.transpose(1, 0, 2)
    weight = w_qkv.transpose(1, 0, 2)
    head = w_head.transpose(1, 0)

    lead, body = modulate(current, levels, mods)
    leads = [lead] + spread(lead, direct(table), place)
    held = spread(body, table[:-1], place)
    half = line // 2
    for part in (leads[:half], leads[half:]):
        pair = over_core(jnp.concatenate(part, 0))
        leads = leads + jnp.split(pair, half, 0)
    lead_part = project(leads, qk_gain, weight)
    packed, origins = from_earlier(lead_part[1:])

    last = take(table[-1], body, [after(tile, lead_part) for tile in held], place)
    first = [body] + [after(tile, lead_part) for tile in held]
    across = over_core(jnp.concatenate(first, 0))
    early_part = project([body] + held + [across], qk_gain, weight)
    last = after(last, early_part)
    late_part = project([last, over_core(last)], qk_gain, weight)
    parts = [lead_part, early_part, late_part]

    def at(lane, slot):
        if slot < line - 1:
            return 1, (lane * (line - 1) + slot) * BODY
        return 2, lane * BODY

    def attended(tail, parts):
        cuts = []
        for lane in range(CORES):
            for slot in range(line):
                part, begin = at(lane, slot)
                middle = begin + BODY - END
                if tail:
                    cuts.append((part, middle, middle + END))
                else:
                    begin_lead = (lane * line + slot) * LEAD
                    cuts.append((0, begin_lead, begin_lead + LEAD))
                    cuts.append((part, begin, middle))
        return attend(cuts, parts, packed, origins, clip, visible, frame_counts, w_out)

    at_place = place.astype(jnp.int32).reshape(1)
    own_end, end_sent = passed_back(output(*attended(True, parts), line), table, at_place)
    parts[-1] = after(parts[-1], own_end[0])
    *terms, last = output(*attended(False, parts), line)
    own, sent = passed_back(terms + [after(last, *end_sent)], table, at_place)

    end_sums = own_end + sent_home(end_sent, table)
    end, end_feats = end_rows(current, levels, mods, head, end_sums)
    earlier = from_behind(end_feats[END - HALO :], "span", 1)
    sums = own + sent_home([after(term, end_feats) for term in sent], table)
    denoised, decoded = finish(
        current, levels, mods, head, conv_w, earlier, end, end_feats, sums
    )
    return (denoised[None], decoded[None])


def solution(mesh):
    placed = (
        P("span", "tok", None),
        P("span"),
        P(),
        P(),
        P(),
        P(None, None, "tok"),
        P(None, "tok"),
        P("tok", None),
        P(),
        P(),
    )
    return jax.shard_map(
        per_device,
        mesh=mesh,
        in_specs=placed,
        out_specs=(P("span", "tok", None), P("span", "tok", None)),
        check_vma=False,
    )
```

```python
import functools

import jax
import jax.numpy as jnp
from jax import lax
from jax.experimental import pallas as pl
from jax.experimental.pallas import tpu as pltpu
from jax.sharding import PartitionSpec as P

HD = 128
FRAMES = 8
KEEP = 2
SPOTS = 8
TOK_DEV = 64
CORES = 2
LEAD = KEEP * SPOTS
HALO = 2 * SPOTS
BODY = TOK_DEV - LEAD
END = 32
REST = TOK_DEV - END


EPS = 1e-06
NEG = -1e30
LOG2E = 1.4426950408889634
MIB = 1 << 20


def routes(line):
    if line == 4:
        return [
            ([(0, 2), (2, 3), (3, 1), (1, 0)], None),
            ([(0, 1), (1, 3), (3, 2), (2, 0)], None),
            ([(0, 1), (1, 0), (2, 3), (3, 2)], (1, 0, 0, 1)),
        ]
    return [([(i, (i + by) % line) for i in range(line)], None) for by in range(1, line)]


def direct(table):
    def origin(place, relay):
        if relay is None:
            return place
        return next(a for a, b in table[relay[place]][0] if b == place)

    return [([(origin(a, relay), b) for a, b in pairs], None) for pairs, relay in table]


def lanes(pairs):
    return [(a * CORES + c, b * CORES + c) for a, b in pairs for c in range(CORES)]


def back(pairs):
    return [(b, a) for a, b in pairs]


def after(array, *others):
    return lax.optimization_barrier((array,) + others)[0]


def over_core(array):
    devices = lax.axis_size("tok")
    return lax.ppermute(array, "tok", [(i, i ^ 1) for i in range(devices)])


def from_behind(array, axis, by):
    devices = lax.axis_size(axis)
    pairs = [(i, i + by) for i in range(devices) if 0 <= i + by < devices]
    return lax.ppermute(array, axis, pairs)


def from_earlier(array):
    devices = lax.axis_size("span")
    if devices != 4:
        steps = range(1, devices)
        came = [from_behind(array, "span", by) for by in steps]
        return came, [lambda me, by=by: me - by for by in steps]
    beside = lax.ppermute(array, "span", [(0, 1), (2, 3)])
    behind = lax.ppermute(array, "span", [(0, 2), (1, 3)])
    across = lax.ppermute(after(behind, beside), "span", [(3, 2), (2, 3)])
    return [beside, behind, across], [
        lambda me: jnp.where(me % 2 == 1, me - 1, -1),
        lambda me: me - 2,
        lambda me: jnp.where(me % 2 == 1, me - 3, me - 1),
    ]


def vmem():
    return pl.BlockSpec(memory_space=pltpu.VMEM)


def smem():
    return pl.BlockSpec(memory_space=pltpu.SMEM)


def hbm():
    return pl.BlockSpec(memory_space=pltpu.HBM)


def in_hbm(array):
    return pltpu.with_memory_space_constraint(array, pltpu.HBM)


def in_vmem(array):
    return pltpu.with_memory_space_constraint(array, pltpu.VMEM)


CHEAP = pl.CostEstimate(flops=1, bytes_accessed=1, transcendentals=0)


def params(mib):
    return pltpu.CompilerParams(vmem_limit_bytes=mib * MIB)


def modulate_kernel(level, rows, table, lead, body, held, mods, sems):
    base = pl.multiple_of(level[0] // 8 * 8, 8)
    copies = [
        pltpu.make_async_copy(rows, held, sems.at[0]),
        pltpu.make_async_copy(table.at[pl.ds(0, 2), pl.ds(base, 8)], mods, sems.at[1]),
    ]
    for copy in copies:
        copy.start()
    for copy in copies:
        copy.wait()
    at = pl.ds(level[0] % 8, 1)
    begin = 0
    for out in (lead, body):
        values = held[begin : begin + out.shape[0]].astype(jnp.float32)
        centre = values - jnp.mean(values, -1, keepdims=True)
        spread = jnp.mean(centre * centre, -1, keepdims=True)
        out[...] = (
            centre * lax.rsqrt(spread + EPS) * (1.0 + mods[1, at, :]) + mods[0, at, :]
        ).astype(jnp.bfloat16)
        begin += out.shape[0]


def modulate(latents, levels, table):
    rows, width = latents.shape
    return pl.pallas_call(
        modulate_kernel,
        in_specs=[smem(), hbm(), hbm()],
        out_specs=[vmem()] * 2,
        out_shape=[
            jax.ShapeDtypeStruct((part, width), jnp.bfloat16) for part in (LEAD, rows - LEAD)
        ],
        scratch_shapes=[
            pltpu.VMEM((rows, width), jnp.bfloat16),
            pltpu.VMEM((2, 8, width), jnp.float32),
            pltpu.SemaphoreType.DMA((2,)),
        ],
        compiler_params=params(8),
        cost_estimate=CHEAP,
    )(levels, in_hbm(latents), in_hbm(table))


def project_kernel(count, load, *refs):
    tiles, (gain, weight, out), refs = refs[:count], refs[count : count + 3], refs[count + 3 :]
    copies = []
    if load:
        kept, held, sems = refs
        for part in range(3):
            copies.append(pltpu.make_async_copy(weight.at[part], kept.at[part], sems.at[part]))
            copies[-1].start()
        weight = kept
    else:
        (held,) = refs
    begin = 0
    for tile in tiles:
        held[begin : begin + tile.shape[0]] = tile[...]
        begin += tile.shape[0]
    for part in range(3):
        if load:
            copies[part].wait()
        proj = jnp.dot(held[...], weight[part], preferred_element_type=jnp.float32)
        if part == 2:
            out[part] = proj.astype(jnp.bfloat16)
            continue
        for h in range(proj.shape[1] // HD):
            cut = slice(h * HD, (h + 1) * HD)
            head = proj[:, cut]
            square = jnp.mean(head * head, -1, keepdims=True)
            out[part, :, cut] = (
                head * lax.rsqrt(square + EPS) * gain[part : part + 1, cut]
            ).astype(jnp.bfloat16)


def project(tiles, gain, weight, load=True):
    rows = sum(tile.shape[0] for tile in tiles)
    width, cols = weight.shape[1:]
    scratch = [pltpu.VMEM((rows, width), jnp.bfloat16)]
    if load:
        scratch = [pltpu.VMEM(weight.shape, weight.dtype)] + scratch
        scratch.append(pltpu.SemaphoreType.DMA((3,)))
    return pl.pallas_call(
        functools.partial(project_kernel, len(tiles), load),
        in_specs=[vmem()] * (len(tiles) + 1) + [hbm() if load else vmem()],
        out_specs=vmem(),
        out_shape=jax.ShapeDtypeStruct((3, rows, cols), jnp.bfloat16),
        scratch_shapes=scratch,
        compiler_params=params((18 if load else 7) + rows // 64 // 8),
        cost_estimate=CHEAP,
    )(*tiles, gain, in_hbm(weight) if load else weight)


def attend_kernel(cuts, own, origins, clip, visible, counts, *refs):
    parts = refs[:own]
    behind = len(origins)
    packed = refs[own : own + behind]
    weight, out, kept, sem = refs[own + behind :]
    copy = pltpu.make_async_copy(weight, kept, sem)
    copy.start()
    me = clip[0]
    scale = HD ** (-0.5) * LOG2E
    bias = []
    for origin, block in zip(origins, packed):
        source = origin(me)
        at = jnp.maximum(source, 0)
        limit = jnp.where((source >= 0) & (visible[me, at] == 1), counts[at], 0)
        row = lax.broadcasted_iota(jnp.int32, (1, block.shape[1]), 1)
        bias.append(jnp.where(row % LEAD // SPOTS < limit, 0.0, NEG))
    heads = [slice(h * HD, (h + 1) * HD) for h in range(out.shape[1] // HD)]
    scores = []
    for cut in heads:
        query = jnp.concatenate(
            [parts[part][0, begin:end, cut] for part, begin, end in cuts], 0
        )
        keys = [(ref[1, :, cut], None) for ref in parts]
        keys += [(ref[0, :, cut], add) for ref, add in zip(packed, bias)]
        row = []
        for key, add in keys:
            score = lax.dot_general(
                query, key, (((1,), (1,)), ((), ())), preferred_element_type=jnp.float32
            )
            row.append(score if add is None else score + add)
        scores.append(row)
    terms, totals = [], []
    for row in scores:
        best = functools.reduce(jnp.maximum, [jnp.max(score, -1, keepdims=True) for score in row])
        row = [jnp.exp2((score - best) * scale) for score in row]
        totals.append(sum(jnp.sum(term, -1, keepdims=True) for term in row))
        terms.append([term.astype(jnp.bfloat16) for term in row])
    for cut, row, total in zip(heads, terms, totals):
        values = [ref[2, :, cut] for ref in parts]
        values += [ref[1, :, cut] for ref in packed]
        acc = sum(
            jnp.dot(term, value, preferred_element_type=jnp.float32)
            for term, value in zip(row, values)
        )
        out[:, cut] = (acc / total).astype(jnp.bfloat16)
    copy.wait()


def attend(cuts, parts, packed, origins, clip, visible, counts, weight):
    cols = parts[0].shape[2]
    seen = sum(part.shape[1] for part in parts)
    seen += sum(block.shape[1] for block in packed)
    rows = sum(end - begin for _, begin, end in cuts)
    return pl.pallas_call(
        functools.partial(attend_kernel, cuts, len(parts), origins),
        in_specs=[smem()] * 3 + [vmem()] * (len(parts) + len(packed)) + [hbm()],
        out_specs=[vmem()] * 2,
        out_shape=[
            jax.ShapeDtypeStruct((rows, cols), jnp.bfloat16),
            pltpu.VMEM(weight.shape, weight.dtype),
        ],
        scratch_shapes=[pltpu.SemaphoreType.DMA],
        compiler_params=params(max(10, 12 * rows * seen * cols // HD // MIB)),
        cost_estimate=CHEAP,
    )(clip, visible, counts, *parts, *packed, in_hbm(weight))


def output_kernel(attended, weight, *outs):
    unit = 512
    for column in range(0, weight.shape[1], unit):
        cut = slice(column, column + unit)
        term = jnp.dot(attended[...], weight[:, cut], preferred_element_type=jnp.float32)
        term = term.astype(jnp.bfloat16)
        begin = 0
        for out in outs:
            out[:, cut] = term[begin : begin + out.shape[0]]
            begin += out.shape[0]


def output(attended, weight, slots):
    rows, cols = attended.shape
    width = weight.shape[1]
    unit = rows // (CORES * slots)
    sizes = [unit] * slots + [unit * (slots - 1), unit]
    return pl.pallas_call(
        output_kernel,
        in_specs=[vmem()] * 2,
        out_specs=[vmem()] * len(sizes),
        out_shape=[jax.ShapeDtypeStruct((size, width), jnp.bfloat16) for size in sizes],
        compiler_params=params(10),
        cost_estimate=CHEAP,
    )(attended, in_vmem(weight))


def fold(rows, gate, terms):
    size = rows.shape[0]
    total = functools.reduce(lambda a, b: a + b, [term[:size].astype(jnp.float32) for term in terms])
    return (rows.astype(jnp.float32) + gate * total).astype(jnp.bfloat16)


def project_head(rows, head):
    return lax.dot_general(
        rows, head, (((1,), (1,)), ((), ())), preferred_element_type=jnp.float32
    ).astype(jnp.bfloat16)


def end_kernel(level, rows, table, head, *refs):
    terms, (new, feats) = refs[:-2], refs[-2:]
    gate = table[2, pl.ds(level[0], 1), :]
    new[...] = fold(rows[REST:, :], gate, terms)
    feats[...] = project_head(new[...], head[...])


def end_rows(latents, levels, table, head, terms):
    rows, width = terms[0].shape
    channels = head.shape[0]
    return pl.pallas_call(
        end_kernel,
        in_specs=[smem()] + [vmem()] * (3 + len(terms)),
        out_specs=[vmem()] * 2,
        out_shape=[
            jax.ShapeDtypeStruct((rows, width), jnp.bfloat16),
            jax.ShapeDtypeStruct((rows, channels), jnp.bfloat16),
        ],
        compiler_params=params(8),
        cost_estimate=CHEAP,
    )(levels, latents, table, head, *terms)


def finish_kernel(level, rows, table, head, weight, earlier, end, end_feats, *refs):
    terms, (denoised, decoded) = refs[:-2], refs[-2:]
    gate = table[2, pl.ds(level[0], 1), :]
    new = fold(rows[:REST, :], gate, terms)
    denoised[:REST] = new
    denoised[REST:] = end[...]
    feats = project_head(new, head[...])
    sequence = jnp.concatenate([earlier[...], feats, end_feats[...]], 0)
    conv = jnp.zeros(decoded.shape, jnp.float32)
    for tap in range(3):
        begin = HALO - tap * SPOTS
        conv = conv + jnp.dot(
            sequence[begin : begin + TOK_DEV], weight[tap], preferred_element_type=jnp.float32
        )
    decoded[...] = (conv / (1.0 + jnp.exp(-conv))).astype(jnp.bfloat16)


def finish(latents, levels, table, head, weight, earlier, end, end_feats, terms):
    rows, width = latents.shape
    return pl.pallas_call(
        finish_kernel,
        in_specs=[smem()] + [vmem()] * (7 + len(terms)),
        out_specs=[vmem()] * 2,
        out_shape=[
            jax.ShapeDtypeStruct((rows, width), jnp.bfloat16),
            jax.ShapeDtypeStruct((rows, weight.shape[2]), jnp.bfloat16),
        ],
        compiler_params=params(8),
        cost_estimate=CHEAP,
    )(levels, latents, table, head, weight, earlier, end, end_feats, *terms)


def passes(relay, slot, place):
    return functools.reduce(
        lambda a, b: a | b, [place == at for at, kept in enumerate(relay) if kept == slot]
    )


def masks(table, place):
    return [
        [passes(relay, slot, place) for slot in sorted(set(relay))[1:]] if relay else []
        for _, relay in table
    ]


def take(entry, tile, held, mask):
    pairs, relay = entry
    if relay is not None:
        first, *others = sorted(set(relay))
        tile = held[first]
        for slot, here in zip(others, mask):
            tile = jnp.where(here, held[slot], tile)
    return lax.ppermute(tile, "tok", lanes(pairs))


def spread(tile, table):
    return [take(entry, tile, [], []) for entry in table]


def merge_kernel(groups, count, place, *refs):
    arrays, outs = refs[:count], refs[count:]
    for out, group in zip(outs, groups):
        rows = out.shape[0]
        sums = 0.0
        for which, block, places in group:
            term = arrays[which][block * rows : (block + 1) * rows].astype(jnp.float32)
            if places is not None:
                here = functools.reduce(lambda a, b: a | b, [place[0] == p for p in places])
                term = jnp.where(here, term, 0.0)
            sums = sums + term
        out[...] = sums.astype(jnp.bfloat16)


def merge(place, arrays, groups):
    unit = arrays[0].shape
    return pl.pallas_call(
        functools.partial(merge_kernel, groups, len(arrays)),
        in_specs=[smem()] + [vmem()] * len(arrays),
        out_specs=[vmem()] * len(groups),
        out_shape=[jax.ShapeDtypeStruct(unit, jnp.bfloat16)] * len(groups),
        compiler_params=params(8),
        cost_estimate=CHEAP,
    )(place, *arrays)


def passed_back(terms, table, place):
    *mine, others, last = terms
    last = over_core(last)
    others = over_core(others)
    final = len(table) - 1
    passed = []
    for slot, (pairs, relay) in enumerate(table):
        if relay is not None:
            theirs = (last, 0) if slot == final else (others, slot + 1)
            (sums,) = merge(place, [mine[slot + 1], theirs[0]], [[(0, 0, None), (1, theirs[1], None)]])
            came = lax.ppermute(sums, "tok", lanes(back(pairs)))
            passed.append((came, relay))
    arrays = mine[1:] + [others, last] + [came for came, _ in passed]
    groups = []
    for slot, (_, relay) in enumerate(table):
        if relay is not None:
            continue
        group = [(slot, 0, None)]
        group.append((final + 2, 0, None) if slot == final else (final + 1, slot + 1, None))
        for i, (_, kept) in enumerate(passed):
            places = [at for at, which in enumerate(kept) if which == slot]
            group.append((final + 3 + i, 0, places))
        groups.append(group)
    return [mine[0], others], merge(place, arrays, groups)


def sent_home(sent, table):
    direct = [pairs for pairs, relay in table if relay is None]
    return [
        lax.ppermute(term, "tok", lanes(back(pairs))) for term, pairs in zip(sent, direct)
    ]


def per_device(
    latents, levels, visible, frame_counts, modulation, w_qkv, qk_gain, w_out, w_head, conv_w
):
    current = latents[0]
    line = lax.axis_size("tok") // CORES
    place = lax.axis_index("tok") // CORES
    clip = lax.axis_index("span").astype(jnp.int32).reshape(1)
    table = routes(line)
    mods = modulation.transpose(1, 0, 2)
    weight = w_qkv.transpose(1, 0, 2)
    head = w_head.transpose(1, 0)

    lead, body = modulate(current, levels, mods)
    at_place = place.astype(jnp.int32).reshape(1)
    lead, body, clip, at_place, mask = lax.optimization_barrier(
        (lead, body, clip, at_place, masks(table, place))
    )
    leads = [lead] + spread(lead, direct(table))
    held = spread(body, table[:-1])
    half = line // 2
    for part in (leads[:half], leads[half:]):
        pair = over_core(jnp.concatenate(part, 0))
        leads = leads + jnp.split(pair, half, 0)
    lead_part = project(leads, qk_gain, weight)
    packed, origins = from_earlier(lead_part[1:])

    last = take(table[-1], body, [after(tile, *packed[:2]) for tile in held], mask[-1])
    first = [body] + [after(tile, lead_part) for tile in held]
    across = over_core(jnp.concatenate(first, 0))
    early_part = project([body] + held + [across], qk_gain, weight, False)
    last = after(last, early_part, *packed)
    late_part = project([last, over_core(last)], qk_gain, weight, False)
    parts = [lead_part, early_part, late_part]

    def at(lane, slot):
        if slot < line - 1:
            return 1, (lane * (line - 1) + slot) * BODY
        return 2, lane * BODY

    def attended(tail, parts):
        cuts = []
        for lane in range(CORES):
            for slot in range(line):
                part, begin = at(lane, slot)
                middle = begin + BODY - END
                if tail:
                    cuts.append((part, middle, middle + END))
                else:
                    begin_lead = (lane * line + slot) * LEAD
                    cuts.append((0, begin_lead, begin_lead + LEAD))
                    cuts.append((part, begin, middle))
        return attend(cuts, parts, packed, origins, clip, visible, frame_counts, w_out)

    own_end, end_sent = passed_back(output(*attended(True, parts), line), table, at_place)
    parts[-1] = after(parts[-1], own_end[0])
    *terms, last = output(*attended(False, parts), line)
    own, sent = passed_back(terms + [after(last, *end_sent)], table, at_place)

    end_sums = own_end + sent_home(end_sent, table)
    end, end_feats = end_rows(current, levels, mods, head, end_sums)
    earlier = from_behind(end_feats[END - HALO :], "span", 1)
    sums = own + sent_home([after(term, end_feats) for term in sent], table)
    denoised, decoded = finish(
        current, levels, mods, head, conv_w, earlier, end, end_feats, sums
    )
    return (denoised[None], decoded[None])


def solution(mesh):
    placed = (
        P("span", "tok", None),
        P("span"),
        P(),
        P(),
        P(),
        P(None, None, "tok"),
        P(None, "tok"),
        P("tok", None),
        P(),
        P(),
    )
    return jax.shard_map(
        per_device,
        mesh=mesh,
        in_specs=placed,
        out_specs=(P("span", "tok", None), P("span", "tok", None)),
        check_vma=False,
    )
```

```python
import functools

import jax
import jax.numpy as jnp
from jax import lax
from jax.experimental import pallas as pl
from jax.experimental.pallas import tpu as pltpu
from jax.sharding import PartitionSpec as P

HD = 128
FRAMES = 8
KEEP = 2
SPOTS = 8
TOK_DEV = 64
CORES = 2
LEAD = KEEP * SPOTS
HALO = 2 * SPOTS
BODY = TOK_DEV - LEAD
END = 32
REST = TOK_DEV - END


EPS = 1e-06
NEG = -1e30
LOG2E = 1.4426950408889634
MIB = 1 << 20


def routes(line):
    if line == 4:
        return [
            ([(0, 2), (2, 3), (3, 1), (1, 0)], None),
            ([(0, 1), (1, 3), (3, 2), (2, 0)], None),
            ([(0, 1), (1, 0), (2, 3), (3, 2)], (1, 0, 0, 1)),
        ]
    return [([(i, (i + by) % line) for i in range(line)], None) for by in range(1, line)]


def direct(table):
    def origin(place, relay):
        if relay is None:
            return place
        return next(a for a, b in table[relay[place]][0] if b == place)

    return [([(origin(a, relay), b) for a, b in pairs], None) for pairs, relay in table]


def lanes(pairs):
    return [(a * CORES + c, b * CORES + c) for a, b in pairs for c in range(CORES)]


def back(pairs):
    return [(b, a) for a, b in pairs]


def after(array, *others):
    return lax.optimization_barrier((array,) + others)[0]


def over_core(array):
    devices = lax.axis_size("tok")
    return lax.ppermute(array, "tok", [(i, i ^ 1) for i in range(devices)])


def from_behind(array, axis, by):
    devices = lax.axis_size(axis)
    pairs = [(i, i + by) for i in range(devices) if 0 <= i + by < devices]
    return lax.ppermute(array, axis, pairs)


def from_earlier(array):
    devices = lax.axis_size("span")
    if devices != 4:
        steps = range(1, devices)
        came = [from_behind(array, "span", by) for by in steps]
        return came, [lambda me, by=by: me - by for by in steps]
    beside = lax.ppermute(array, "span", [(0, 1), (2, 3)])
    behind = lax.ppermute(array, "span", [(0, 2), (1, 3)])
    across = lax.ppermute(after(behind, beside), "span", [(3, 2), (2, 3)])
    return [beside, behind, across], [
        lambda me: jnp.where(me % 2 == 1, me - 1, -1),
        lambda me: me - 2,
        lambda me: jnp.where(me % 2 == 1, me - 3, me - 1),
    ]


def vmem():
    return pl.BlockSpec(memory_space=pltpu.VMEM)


def smem():
    return pl.BlockSpec(memory_space=pltpu.SMEM)


def hbm():
    return pl.BlockSpec(memory_space=pltpu.HBM)


def in_hbm(array):
    return pltpu.with_memory_space_constraint(array, pltpu.HBM)


def in_vmem(array):
    return pltpu.with_memory_space_constraint(array, pltpu.VMEM)


CHEAP = pl.CostEstimate(flops=1, bytes_accessed=1, transcendentals=0)


def params(mib):
    return pltpu.CompilerParams(vmem_limit_bytes=mib * MIB)


def modulate_kernel(level, rows, table, lead, body, held, mods, sems):
    base = pl.multiple_of(level[0] // 8 * 8, 8)
    copies = [
        pltpu.make_async_copy(rows, held, sems.at[0]),
        pltpu.make_async_copy(table.at[pl.ds(0, 2), pl.ds(base, 8)], mods, sems.at[1]),
    ]
    for copy in copies:
        copy.start()
    for copy in copies:
        copy.wait()
    at = pl.ds(level[0] % 8, 1)
    begin = 0
    for out in (lead, body):
        values = held[begin : begin + out.shape[0]].astype(jnp.float32)
        centre = values - jnp.mean(values, -1, keepdims=True)
        spread = jnp.mean(centre * centre, -1, keepdims=True)
        out[...] = (
            centre * lax.rsqrt(spread + EPS) * (1.0 + mods[1, at, :]) + mods[0, at, :]
        ).astype(jnp.bfloat16)
        begin += out.shape[0]


def modulate(latents, levels, table):
    rows, width = latents.shape
    return pl.pallas_call(
        modulate_kernel,
        in_specs=[smem(), hbm(), hbm()],
        out_specs=[vmem()] * 2,
        out_shape=[
            jax.ShapeDtypeStruct((part, width), jnp.bfloat16) for part in (LEAD, rows - LEAD)
        ],
        scratch_shapes=[
            pltpu.VMEM((rows, width), jnp.bfloat16),
            pltpu.VMEM((2, 8, width), jnp.float32),
            pltpu.SemaphoreType.DMA((2,)),
        ],
        compiler_params=params(8),
        cost_estimate=CHEAP,
    )(levels, in_hbm(latents), in_hbm(table))


def project_kernel(count, load, *refs):
    tiles, (gain, weight, out), refs = refs[:count], refs[count : count + 3], refs[count + 3 :]
    copies = []
    if load:
        kept, held, sems = refs
        for part in range(3):
            copies.append(pltpu.make_async_copy(weight.at[part], kept.at[part], sems.at[part]))
            copies[-1].start()
        weight = kept
    else:
        (held,) = refs
    begin = 0
    for tile in tiles:
        held[begin : begin + tile.shape[0]] = tile[...]
        begin += tile.shape[0]
    for part in range(3):
        if load:
            copies[part].wait()
        proj = jnp.dot(held[...], weight[part], preferred_element_type=jnp.float32)
        if part == 2:
            out[part] = proj.astype(jnp.bfloat16)
            continue
        for h in range(proj.shape[1] // HD):
            cut = slice(h * HD, (h + 1) * HD)
            head = proj[:, cut]
            square = jnp.mean(head * head, -1, keepdims=True)
            out[part, :, cut] = (
                head * lax.rsqrt(square + EPS) * gain[part : part + 1, cut]
            ).astype(jnp.bfloat16)


def project(tiles, gain, weight, load=True):
    rows = sum(tile.shape[0] for tile in tiles)
    width, cols = weight.shape[1:]
    scratch = [pltpu.VMEM((rows, width), jnp.bfloat16)]
    if load:
        scratch = [pltpu.VMEM(weight.shape, weight.dtype)] + scratch
        scratch.append(pltpu.SemaphoreType.DMA((3,)))
    return pl.pallas_call(
        functools.partial(project_kernel, len(tiles), load),
        in_specs=[vmem()] * (len(tiles) + 1) + [hbm() if load else vmem()],
        out_specs=vmem(),
        out_shape=jax.ShapeDtypeStruct((3, rows, cols), jnp.bfloat16),
        scratch_shapes=scratch,
        compiler_params=params((18 if load else 7) + rows // 64 // 8),
        cost_estimate=CHEAP,
    )(*tiles, gain, in_hbm(weight) if load else weight)


def attend_kernel(cuts, own, origins, clip, visible, counts, *refs):
    parts = refs[:own]
    behind = len(origins)
    packed = refs[own : own + behind]
    weight, out, kept, sem = refs[own + behind :]
    copy = pltpu.make_async_copy(weight, kept, sem)
    copy.start()
    me = clip[0]
    scale = HD ** (-0.5) * LOG2E
    bias = []
    for origin, block in zip(origins, packed):
        source = origin(me)
        at = jnp.maximum(source, 0)
        limit = jnp.where((source >= 0) & (visible[me, at] == 1), counts[at], 0)
        row = lax.broadcasted_iota(jnp.int32, (1, block.shape[1]), 1)
        bias.append(jnp.where(row % LEAD // SPOTS < limit, 0.0, NEG))
    heads = [slice(h * HD, (h + 1) * HD) for h in range(out.shape[1] // HD)]
    scores = []
    for cut in heads:
        query = jnp.concatenate(
            [parts[part][0, begin:end, cut] for part, begin, end in cuts], 0
        )
        keys = [(ref[1, :, cut], None) for ref in parts]
        keys += [(ref[0, :, cut], add) for ref, add in zip(packed, bias)]
        row = []
        for key, add in keys:
            score = lax.dot_general(
                query, key, (((1,), (1,)), ((), ())), preferred_element_type=jnp.float32
            )
            row.append(score if add is None else score + add)
        scores.append(row)
    terms, totals = [], []
    for row in scores:
        best = functools.reduce(jnp.maximum, [jnp.max(score, -1, keepdims=True) for score in row])
        row = [jnp.exp2((score - best) * scale) for score in row]
        totals.append(sum(jnp.sum(term, -1, keepdims=True) for term in row))
        terms.append([term.astype(jnp.bfloat16) for term in row])
    for cut, row, total in zip(heads, terms, totals):
        values = [ref[2, :, cut] for ref in parts]
        values += [ref[1, :, cut] for ref in packed]
        acc = sum(
            jnp.dot(term, value, preferred_element_type=jnp.float32)
            for term, value in zip(row, values)
        )
        out[:, cut] = (acc / total).astype(jnp.bfloat16)
    copy.wait()


def attend(cuts, parts, packed, origins, clip, visible, counts, weight):
    cols = parts[0].shape[2]
    seen = sum(part.shape[1] for part in parts)
    seen += sum(block.shape[1] for block in packed)
    rows = sum(end - begin for _, begin, end in cuts)
    return pl.pallas_call(
        functools.partial(attend_kernel, cuts, len(parts), origins),
        in_specs=[smem()] * 3 + [vmem()] * (len(parts) + len(packed)) + [hbm()],
        out_specs=[vmem()] * 2,
        out_shape=[
            jax.ShapeDtypeStruct((rows, cols), jnp.bfloat16),
            pltpu.VMEM(weight.shape, weight.dtype),
        ],
        scratch_shapes=[pltpu.SemaphoreType.DMA],
        compiler_params=params(max(10, 12 * rows * seen * cols // HD // MIB)),
        cost_estimate=CHEAP,
    )(clip, visible, counts, *parts, *packed, in_hbm(weight))


def output_kernel(attended, weight, *outs):
    unit = 512
    for column in range(0, weight.shape[1], unit):
        cut = slice(column, column + unit)
        term = jnp.dot(attended[...], weight[:, cut], preferred_element_type=jnp.float32)
        term = term.astype(jnp.bfloat16)
        begin = 0
        for out in outs:
            out[:, cut] = term[begin : begin + out.shape[0]]
            begin += out.shape[0]


def output(attended, weight, slots):
    rows, cols = attended.shape
    width = weight.shape[1]
    unit = rows // (CORES * slots)
    sizes = [unit] * slots + [unit * (slots - 1), unit]
    return pl.pallas_call(
        output_kernel,
        in_specs=[vmem()] * 2,
        out_specs=[vmem()] * len(sizes),
        out_shape=[jax.ShapeDtypeStruct((size, width), jnp.bfloat16) for size in sizes],
        compiler_params=params(10),
        cost_estimate=CHEAP,
    )(attended, in_vmem(weight))


def fold(rows, gate, terms):
    size = rows.shape[0]
    total = functools.reduce(lambda a, b: a + b, [term[:size].astype(jnp.float32) for term in terms])
    return (rows.astype(jnp.float32) + gate * total).astype(jnp.bfloat16)


def project_head(rows, head):
    return lax.dot_general(
        rows, head, (((1,), (1,)), ((), ())), preferred_element_type=jnp.float32
    ).astype(jnp.bfloat16)


def end_kernel(level, rows, table, head, *refs):
    terms, (new, feats) = refs[:-2], refs[-2:]
    gate = table[2, pl.ds(level[0], 1), :]
    new[...] = fold(rows[REST:, :], gate, terms)
    feats[...] = project_head(new[...], head[...])


def end_rows(latents, levels, table, head, terms):
    rows, width = terms[0].shape
    channels = head.shape[0]
    return pl.pallas_call(
        end_kernel,
        in_specs=[smem()] + [vmem()] * (3 + len(terms)),
        out_specs=[vmem()] * 2,
        out_shape=[
            jax.ShapeDtypeStruct((rows, width), jnp.bfloat16),
            jax.ShapeDtypeStruct((rows, channels), jnp.bfloat16),
        ],
        compiler_params=params(8),
        cost_estimate=CHEAP,
    )(levels, latents, table, head, *terms)


def finish_kernel(level, rows, table, head, weight, earlier, end, end_feats, *refs):
    terms, (denoised, decoded) = refs[:-2], refs[-2:]
    gate = table[2, pl.ds(level[0], 1), :]
    new = fold(rows[:REST, :], gate, terms)
    denoised[:REST] = new
    denoised[REST:] = end[...]
    feats = project_head(new, head[...])
    sequence = jnp.concatenate([earlier[...], feats, end_feats[...]], 0)
    conv = jnp.zeros(decoded.shape, jnp.float32)
    for tap in range(3):
        begin = HALO - tap * SPOTS
        conv = conv + jnp.dot(
            sequence[begin : begin + TOK_DEV], weight[tap], preferred_element_type=jnp.float32
        )
    decoded[...] = (conv / (1.0 + jnp.exp(-conv))).astype(jnp.bfloat16)


def finish(latents, levels, table, head, weight, earlier, end, end_feats, terms):
    rows, width = latents.shape
    return pl.pallas_call(
        finish_kernel,
        in_specs=[smem()] + [vmem()] * (7 + len(terms)),
        out_specs=[vmem()] * 2,
        out_shape=[
            jax.ShapeDtypeStruct((rows, width), jnp.bfloat16),
            jax.ShapeDtypeStruct((rows, weight.shape[2]), jnp.bfloat16),
        ],
        compiler_params=params(8),
        cost_estimate=CHEAP,
    )(levels, latents, table, head, weight, earlier, end, end_feats, *terms)


def passes(relay, slot, place):
    return functools.reduce(
        lambda a, b: a | b, [place == at for at, kept in enumerate(relay) if kept == slot]
    )


def masks(table, place):
    return [
        [passes(relay, slot, place) for slot in sorted(set(relay))[1:]] if relay else []
        for _, relay in table
    ]


def take(entry, tile, held, mask):
    pairs, relay = entry
    if relay is not None:
        first, *others = sorted(set(relay))
        tile = held[first]
        for slot, here in zip(others, mask):
            tile = jnp.where(here, held[slot], tile)
    return lax.ppermute(tile, "tok", lanes(pairs))


def spread(tile, table):
    return [take(entry, tile, [], []) for entry in table]


def merge_kernel(groups, count, place, *refs):
    arrays, outs = refs[:count], refs[count:]
    for out, group in zip(outs, groups):
        rows = out.shape[0]
        sums = 0.0
        for which, block, places in group:
            term = arrays[which][block * rows : (block + 1) * rows].astype(jnp.float32)
            if places is not None:
                here = functools.reduce(lambda a, b: a | b, [place[0] == p for p in places])
                term = jnp.where(here, term, 0.0)
            sums = sums + term
        out[...] = sums.astype(jnp.bfloat16)


def merge(place, arrays, groups):
    unit = arrays[0].shape
    return pl.pallas_call(
        functools.partial(merge_kernel, groups, len(arrays)),
        in_specs=[smem()] + [vmem()] * len(arrays),
        out_specs=[vmem()] * len(groups),
        out_shape=[jax.ShapeDtypeStruct(unit, jnp.bfloat16)] * len(groups),
        compiler_params=params(8),
        cost_estimate=CHEAP,
    )(place, *arrays)


def passed_back(terms, table, place):
    *mine, others, last = terms
    last = over_core(last)
    others = over_core(others)
    final = len(table) - 1
    passed = []
    for slot, (pairs, relay) in enumerate(table):
        if relay is not None:
            theirs = (last, 0) if slot == final else (others, slot + 1)
            (sums,) = merge(place, [mine[slot + 1], theirs[0]], [[(0, 0, None), (1, theirs[1], None)]])
            came = lax.ppermute(sums, "tok", lanes(back(pairs)))
            passed.append((came, relay))
    arrays = mine[1:] + [others, last] + [came for came, _ in passed]
    groups = []
    for slot, (_, relay) in enumerate(table):
        if relay is not None:
            continue
        group = [(slot, 0, None)]
        group.append((final + 2, 0, None) if slot == final else (final + 1, slot + 1, None))
        for i, (_, kept) in enumerate(passed):
            places = [at for at, which in enumerate(kept) if which == slot]
            group.append((final + 3 + i, 0, places))
        groups.append(group)
    return [mine[0], others], merge(place, arrays, groups)


def sent_home(sent, table):
    direct = [pairs for pairs, relay in table if relay is None]
    return [
        lax.ppermute(term, "tok", lanes(back(pairs))) for term, pairs in zip(sent, direct)
    ]


def per_device(
    latents, levels, visible, frame_counts, modulation, w_qkv, qk_gain, w_out, w_head, conv_w
):
    current = latents[0]
    line = lax.axis_size("tok") // CORES
    place = lax.axis_index("tok") // CORES
    clip = lax.axis_index("span").astype(jnp.int32).reshape(1)
    table = routes(line)
    mods = modulation.transpose(1, 0, 2)
    weight = w_qkv.transpose(1, 0, 2)
    head = w_head.transpose(1, 0)

    lead, body = modulate(current, levels, mods)
    at_place = place.astype(jnp.int32).reshape(1)
    lead, body, clip, at_place, mask = lax.optimization_barrier(
        (lead, body, clip, at_place, masks(table, place))
    )
    leads = [lead] + spread(lead, direct(table))
    held = spread(body, table[:-1])
    half = line // 2
    for part in (leads[:half], leads[half:]):
        pair = over_core(jnp.concatenate(part, 0))
        leads = leads + jnp.split(pair, half, 0)
    lead_part = project(leads, qk_gain, weight)
    packed, origins = from_earlier(lead_part[1:])

    last = take(table[-1], body, [after(tile, lead_part) for tile in held], mask[-1])
    first = [body] + [after(tile, lead_part) for tile in held]
    across = over_core(jnp.concatenate(first, 0))
    early_part = project([body] + held + [across], qk_gain, weight, False)
    last = after(last, early_part, *packed)
    late_part = project([last, over_core(last)], qk_gain, weight, False)
    parts = [lead_part, early_part, late_part]

    def at(lane, slot):
        if slot < line - 1:
            return 1, (lane * (line - 1) + slot) * BODY
        return 2, lane * BODY

    def attended(tail, parts):
        cuts = []
        for lane in range(CORES):
            for slot in range(line):
                part, begin = at(lane, slot)
                middle = begin + BODY - END
                if tail:
                    cuts.append((part, middle, middle + END))
                else:
                    begin_lead = (lane * line + slot) * LEAD
                    cuts.append((0, begin_lead, begin_lead + LEAD))
                    cuts.append((part, begin, middle))
        return attend(cuts, parts, packed, origins, clip, visible, frame_counts, w_out)

    own_end, end_sent = passed_back(output(*attended(True, parts), line), table, at_place)
    parts[-1] = after(parts[-1], own_end[0])
    *terms, last = output(*attended(False, parts), line)
    own, sent = passed_back(terms + [after(last, *end_sent)], table, at_place)

    end_sums = own_end + sent_home(end_sent, table)
    end, end_feats = end_rows(current, levels, mods, head, end_sums)
    earlier = from_behind(end_feats[END - HALO :], "span", 1)
    sums = own + sent_home([after(term, end_feats) for term in sent], table)
    denoised, decoded = finish(
        current, levels, mods, head, conv_w, earlier, end, end_feats, sums
    )
    return (denoised[None], decoded[None])


def solution(mesh):
    placed = (
        P("span", "tok", None),
        P("span"),
        P(),
        P(),
        P(),
        P(None, None, "tok"),
        P(None, "tok"),
        P("tok", None),
        P(),
        P(),
    )
    return jax.shard_map(
        per_device,
        mesh=mesh,
        in_specs=placed,
        out_specs=(P("span", "tok", None), P("span", "tok", None)),
        check_vma=False,
    )
```

```python
import functools

import jax
import jax.numpy as jnp
from jax import lax
from jax.experimental import pallas as pl
from jax.experimental.pallas import tpu as pltpu
from jax.sharding import PartitionSpec as P

HD = 128
FRAMES = 8
KEEP = 2
SPOTS = 8
TOK_DEV = 64
CORES = 2
LEAD = KEEP * SPOTS
HALO = 2 * SPOTS
BODY = TOK_DEV - LEAD
END = 32
REST = TOK_DEV - END


EPS = 1e-06
NEG = -1e30
LOG2E = 1.4426950408889634
MIB = 1 << 20


def routes(line):
    if line == 4:
        return [
            ([(0, 2), (2, 3), (3, 1), (1, 0)], None),
            ([(0, 1), (1, 3), (3, 2), (2, 0)], None),
            ([(0, 1), (1, 0), (2, 3), (3, 2)], (1, 0, 0, 1)),
        ]
    return [([(i, (i + by) % line) for i in range(line)], None) for by in range(1, line)]


def direct(table):
    def origin(place, relay):
        if relay is None:
            return place
        return next(a for a, b in table[relay[place]][0] if b == place)

    return [([(origin(a, relay), b) for a, b in pairs], None) for pairs, relay in table]


def lanes(pairs):
    return [(a * CORES + c, b * CORES + c) for a, b in pairs for c in range(CORES)]


def back(pairs):
    return [(b, a) for a, b in pairs]


def after(array, *others):
    return lax.optimization_barrier((array,) + others)[0]


def over_core(array):
    devices = lax.axis_size("tok")
    return lax.ppermute(array, "tok", [(i, i ^ 1) for i in range(devices)])


def from_behind(array, axis, by):
    devices = lax.axis_size(axis)
    pairs = [(i, i + by) for i in range(devices) if 0 <= i + by < devices]
    return lax.ppermute(array, axis, pairs)


def from_earlier(array):
    devices = lax.axis_size("span")
    if devices != 4:
        steps = range(1, devices)
        came = [from_behind(array, "span", by) for by in steps]
        return came, [lambda me, by=by: me - by for by in steps]
    beside = lax.ppermute(array, "span", [(0, 1), (2, 3)])
    behind = lax.ppermute(array, "span", [(0, 2), (1, 3)])
    across = lax.ppermute(after(behind, beside), "span", [(3, 2), (2, 3)])
    return [beside, behind, across], [
        lambda me: jnp.where(me % 2 == 1, me - 1, -1),
        lambda me: me - 2,
        lambda me: jnp.where(me % 2 == 1, me - 3, me - 1),
    ]


def vmem():
    return pl.BlockSpec(memory_space=pltpu.VMEM)


def smem():
    return pl.BlockSpec(memory_space=pltpu.SMEM)


def hbm():
    return pl.BlockSpec(memory_space=pltpu.HBM)


def in_hbm(array):
    return pltpu.with_memory_space_constraint(array, pltpu.HBM)


def in_vmem(array):
    return pltpu.with_memory_space_constraint(array, pltpu.VMEM)


CHEAP = pl.CostEstimate(flops=1, bytes_accessed=1, transcendentals=0)


def params(mib):
    return pltpu.CompilerParams(vmem_limit_bytes=mib * MIB)


def modulate_kernel(level, rows, table, lead, body, held, mods, sems):
    base = pl.multiple_of(level[0] // 8 * 8, 8)
    copies = [
        pltpu.make_async_copy(rows, held, sems.at[0]),
        pltpu.make_async_copy(table.at[pl.ds(0, 2), pl.ds(base, 8)], mods, sems.at[1]),
    ]
    for copy in copies:
        copy.start()
    for copy in copies:
        copy.wait()
    at = pl.ds(level[0] % 8, 1)
    begin = 0
    for out in (lead, body):
        values = held[begin : begin + out.shape[0]].astype(jnp.float32)
        centre = values - jnp.mean(values, -1, keepdims=True)
        spread = jnp.mean(centre * centre, -1, keepdims=True)
        out[...] = (
            centre * lax.rsqrt(spread + EPS) * (1.0 + mods[1, at, :]) + mods[0, at, :]
        ).astype(jnp.bfloat16)
        begin += out.shape[0]


def modulate(latents, levels, table):
    rows, width = latents.shape
    return pl.pallas_call(
        modulate_kernel,
        in_specs=[smem(), hbm(), hbm()],
        out_specs=[vmem()] * 2,
        out_shape=[
            jax.ShapeDtypeStruct((part, width), jnp.bfloat16) for part in (LEAD, rows - LEAD)
        ],
        scratch_shapes=[
            pltpu.VMEM((rows, width), jnp.bfloat16),
            pltpu.VMEM((2, 8, width), jnp.float32),
            pltpu.SemaphoreType.DMA((2,)),
        ],
        compiler_params=params(8),
        cost_estimate=CHEAP,
    )(levels, in_hbm(latents), in_hbm(table))


def project_kernel(count, load, *refs):
    tiles, (gain, weight, out), refs = refs[:count], refs[count : count + 3], refs[count + 3 :]
    copies = []
    if load:
        kept, held, sems = refs
        for part in range(3):
            copies.append(pltpu.make_async_copy(weight.at[part], kept.at[part], sems.at[part]))
            copies[-1].start()
        weight = kept
    else:
        (held,) = refs
    begin = 0
    for tile in tiles:
        held[begin : begin + tile.shape[0]] = tile[...]
        begin += tile.shape[0]
    for part in range(3):
        if load:
            copies[part].wait()
        proj = jnp.dot(held[...], weight[part], preferred_element_type=jnp.float32)
        if part == 2:
            out[part] = proj.astype(jnp.bfloat16)
            continue
        for h in range(proj.shape[1] // HD):
            cut = slice(h * HD, (h + 1) * HD)
            head = proj[:, cut]
            square = jnp.mean(head * head, -1, keepdims=True)
            out[part, :, cut] = (
                head * lax.rsqrt(square + EPS) * gain[part : part + 1, cut]
            ).astype(jnp.bfloat16)


def project(tiles, gain, weight, load=True):
    rows = sum(tile.shape[0] for tile in tiles)
    width, cols = weight.shape[1:]
    scratch = [pltpu.VMEM((rows, width), jnp.bfloat16)]
    if load:
        scratch = [pltpu.VMEM(weight.shape, weight.dtype)] + scratch
        scratch.append(pltpu.SemaphoreType.DMA((3,)))
    return pl.pallas_call(
        functools.partial(project_kernel, len(tiles), load),
        in_specs=[vmem()] * (len(tiles) + 1) + [hbm() if load else vmem()],
        out_specs=vmem(),
        out_shape=jax.ShapeDtypeStruct((3, rows, cols), jnp.bfloat16),
        scratch_shapes=scratch,
        compiler_params=params((18 if load else 7) + rows // 64 // 8),
        cost_estimate=CHEAP,
    )(*tiles, gain, in_hbm(weight) if load else weight)


def attend_kernel(cuts, own, origins, clip, visible, counts, *refs):
    parts = refs[:own]
    behind = len(origins)
    packed = refs[own : own + behind]
    weight, out, kept, sem = refs[own + behind :]
    copy = pltpu.make_async_copy(weight, kept, sem)
    copy.start()
    me = clip[0]
    scale = HD ** (-0.5) * LOG2E
    bias = []
    for origin, block in zip(origins, packed):
        source = origin(me)
        at = jnp.maximum(source, 0)
        limit = jnp.where((source >= 0) & (visible[me, at] == 1), counts[at], 0)
        row = lax.broadcasted_iota(jnp.int32, (1, block.shape[1]), 1)
        bias.append(jnp.where(row % LEAD // SPOTS < limit, 0.0, NEG))
    heads = [slice(h * HD, (h + 1) * HD) for h in range(out.shape[1] // HD)]
    scores = []
    for cut in heads:
        query = jnp.concatenate(
            [parts[part][0, begin:end, cut] for part, begin, end in cuts], 0
        )
        keys = [(ref[1, :, cut], None) for ref in parts]
        keys += [(ref[0, :, cut], add) for ref, add in zip(packed, bias)]
        row = []
        for key, add in keys:
            score = lax.dot_general(
                query, key, (((1,), (1,)), ((), ())), preferred_element_type=jnp.float32
            )
            row.append(score if add is None else score + add)
        scores.append(row)
    terms, totals = [], []
    for row in scores:
        best = functools.reduce(jnp.maximum, [jnp.max(score, -1, keepdims=True) for score in row])
        row = [jnp.exp2((score - best) * scale) for score in row]
        totals.append(sum(jnp.sum(term, -1, keepdims=True) for term in row))
        terms.append([term.astype(jnp.bfloat16) for term in row])
    for cut, row, total in zip(heads, terms, totals):
        values = [ref[2, :, cut] for ref in parts]
        values += [ref[1, :, cut] for ref in packed]
        acc = sum(
            jnp.dot(term, value, preferred_element_type=jnp.float32)
            for term, value in zip(row, values)
        )
        out[:, cut] = (acc / total).astype(jnp.bfloat16)
    copy.wait()


def attend(cuts, parts, packed, origins, clip, visible, counts, weight):
    cols = parts[0].shape[2]
    seen = sum(part.shape[1] for part in parts)
    seen += sum(block.shape[1] for block in packed)
    rows = sum(end - begin for _, begin, end in cuts)
    return pl.pallas_call(
        functools.partial(attend_kernel, cuts, len(parts), origins),
        in_specs=[smem()] * 3 + [vmem()] * (len(parts) + len(packed)) + [hbm()],
        out_specs=[vmem()] * 2,
        out_shape=[
            jax.ShapeDtypeStruct((rows, cols), jnp.bfloat16),
            pltpu.VMEM(weight.shape, weight.dtype),
        ],
        scratch_shapes=[pltpu.SemaphoreType.DMA],
        compiler_params=params(max(10, 12 * rows * seen * cols // HD // MIB)),
        cost_estimate=CHEAP,
    )(clip, visible, counts, *parts, *packed, in_hbm(weight))


def output_kernel(attended, weight, *outs):
    unit = 512
    for column in range(0, weight.shape[1], unit):
        cut = slice(column, column + unit)
        term = jnp.dot(attended[...], weight[:, cut], preferred_element_type=jnp.float32)
        term = term.astype(jnp.bfloat16)
        begin = 0
        for out in outs:
            out[:, cut] = term[begin : begin + out.shape[0]]
            begin += out.shape[0]


def output(attended, weight, slots):
    rows, cols = attended.shape
    width = weight.shape[1]
    unit = rows // (CORES * slots)
    sizes = [unit] * slots + [unit * (slots - 1), unit]
    return pl.pallas_call(
        output_kernel,
        in_specs=[vmem()] * 2,
        out_specs=[vmem()] * len(sizes),
        out_shape=[jax.ShapeDtypeStruct((size, width), jnp.bfloat16) for size in sizes],
        compiler_params=params(10),
        cost_estimate=CHEAP,
    )(attended, in_vmem(weight))


def fold(rows, gate, terms):
    size = rows.shape[0]
    total = functools.reduce(lambda a, b: a + b, [term[:size].astype(jnp.float32) for term in terms])
    return (rows.astype(jnp.float32) + gate * total).astype(jnp.bfloat16)


def project_head(rows, head):
    return lax.dot_general(
        rows, head, (((1,), (1,)), ((), ())), preferred_element_type=jnp.float32
    ).astype(jnp.bfloat16)


def end_kernel(level, rows, table, head, *refs):
    terms, (new, feats) = refs[:-2], refs[-2:]
    gate = table[2, pl.ds(level[0], 1), :]
    new[...] = fold(rows[REST:, :], gate, terms)
    feats[...] = project_head(new[...], head[...])


def end_rows(latents, levels, table, head, terms):
    rows, width = terms[0].shape
    channels = head.shape[0]
    return pl.pallas_call(
        end_kernel,
        in_specs=[smem()] + [vmem()] * (3 + len(terms)),
        out_specs=[vmem()] * 2,
        out_shape=[
            jax.ShapeDtypeStruct((rows, width), jnp.bfloat16),
            jax.ShapeDtypeStruct((rows, channels), jnp.bfloat16),
        ],
        compiler_params=params(8),
        cost_estimate=CHEAP,
    )(levels, latents, table, head, *terms)


def finish_kernel(level, rows, table, head, weight, earlier, end, end_feats, *refs):
    terms, (denoised, decoded) = refs[:-2], refs[-2:]
    gate = table[2, pl.ds(level[0], 1), :]
    new = fold(rows[:REST, :], gate, terms)
    denoised[:REST] = new
    denoised[REST:] = end[...]
    feats = project_head(new, head[...])
    sequence = jnp.concatenate([earlier[...], feats, end_feats[...]], 0)
    conv = jnp.zeros(decoded.shape, jnp.float32)
    for tap in range(3):
        begin = HALO - tap * SPOTS
        conv = conv + jnp.dot(
            sequence[begin : begin + TOK_DEV], weight[tap], preferred_element_type=jnp.float32
        )
    decoded[...] = (conv / (1.0 + jnp.exp(-conv))).astype(jnp.bfloat16)


def finish(latents, levels, table, head, weight, earlier, end, end_feats, terms):
    rows, width = latents.shape
    return pl.pallas_call(
        finish_kernel,
        in_specs=[smem()] + [vmem()] * (7 + len(terms)),
        out_specs=[vmem()] * 2,
        out_shape=[
            jax.ShapeDtypeStruct((rows, width), jnp.bfloat16),
            jax.ShapeDtypeStruct((rows, weight.shape[2]), jnp.bfloat16),
        ],
        compiler_params=params(8),
        cost_estimate=CHEAP,
    )(levels, latents, table, head, weight, earlier, end, end_feats, *terms)


def passes(relay, slot, place):
    return functools.reduce(
        lambda a, b: a | b, [place == at for at, kept in enumerate(relay) if kept == slot]
    )


def masks(table, place):
    return [
        [passes(relay, slot, place) for slot in sorted(set(relay))[1:]] if relay else []
        for _, relay in table
    ]


def take(entry, tile, held, mask):
    pairs, relay = entry
    if relay is not None:
        first, *others = sorted(set(relay))
        tile = held[first]
        for slot, here in zip(others, mask):
            tile = jnp.where(here, held[slot], tile)
    return lax.ppermute(tile, "tok", lanes(pairs))


def spread(tile, table):
    return [take(entry, tile, [], []) for entry in table]


def merge_kernel(groups, count, place, *refs):
    arrays, outs = refs[:count], refs[count:]
    for out, group in zip(outs, groups):
        rows = out.shape[0]
        sums = 0.0
        for which, block, places in group:
            term = arrays[which][block * rows : (block + 1) * rows].astype(jnp.float32)
            if places is not None:
                here = functools.reduce(lambda a, b: a | b, [place[0] == p for p in places])
                term = jnp.where(here, term, 0.0)
            sums = sums + term
        out[...] = sums.astype(jnp.bfloat16)


def merge(place, arrays, groups):
    unit = arrays[0].shape
    return pl.pallas_call(
        functools.partial(merge_kernel, groups, len(arrays)),
        in_specs=[smem()] + [vmem()] * len(arrays),
        out_specs=[vmem()] * len(groups),
        out_shape=[jax.ShapeDtypeStruct(unit, jnp.bfloat16)] * len(groups),
        compiler_params=params(8),
        cost_estimate=CHEAP,
    )(place, *arrays)


def passed_back(terms, table, place):
    *mine, others, last = terms
    last = over_core(last)
    others = over_core(others)
    final = len(table) - 1
    passed = []
    for slot, (pairs, relay) in enumerate(table):
        if relay is not None:
            theirs = (last, 0) if slot == final else (others, slot + 1)
            (sums,) = merge(place, [mine[slot + 1], theirs[0]], [[(0, 0, None), (1, theirs[1], None)]])
            came = lax.ppermute(sums, "tok", lanes(back(pairs)))
            passed.append((came, relay))
    arrays = mine[1:] + [others, last] + [came for came, _ in passed]
    groups = []
    for slot, (_, relay) in enumerate(table):
        if relay is not None:
            continue
        group = [(slot, 0, None)]
        group.append((final + 2, 0, None) if slot == final else (final + 1, slot + 1, None))
        for i, (_, kept) in enumerate(passed):
            places = [at for at, which in enumerate(kept) if which == slot]
            group.append((final + 3 + i, 0, places))
        groups.append(group)
    return [mine[0], others], merge(place, arrays, groups)


def sent_home(sent, table):
    direct = [pairs for pairs, relay in table if relay is None]
    return [
        lax.ppermute(term, "tok", lanes(back(pairs))) for term, pairs in zip(sent, direct)
    ]


def per_device(
    latents, levels, visible, frame_counts, modulation, w_qkv, qk_gain, w_out, w_head, conv_w
):
    current = latents[0]
    line = lax.axis_size("tok") // CORES
    place = lax.axis_index("tok") // CORES
    clip = lax.axis_index("span").astype(jnp.int32).reshape(1)
    table = routes(line)
    mods = modulation.transpose(1, 0, 2)
    weight = w_qkv.transpose(1, 0, 2)
    head = w_head.transpose(1, 0)

    lead, body = modulate(current, levels, mods)
    at_place = place.astype(jnp.int32).reshape(1)
    lead, body, clip, at_place, mask = lax.optimization_barrier(
        (lead, body, clip, at_place, masks(table, place))
    )
    leads = [lead] + spread(lead, direct(table))
    held = spread(body, table[:-1])
    half = line // 2
    for part in (leads[:half], leads[half:]):
        pair = over_core(jnp.concatenate(part, 0))
        leads = leads + jnp.split(pair, half, 0)
    lead_part = project(leads, qk_gain, weight)
    packed, origins = from_earlier(lead_part[1:])

    last = take(table[-1], body, [after(tile, lead_part) for tile in held], mask[-1])
    first = [body] + held
    across = over_core(jnp.concatenate(first, 0))
    early_part = project([body] + held + [across], qk_gain, weight, False)
    last = after(last, early_part, *packed)
    late_part = project([last, over_core(last)], qk_gain, weight, False)
    parts = [lead_part, early_part, late_part]

    def at(lane, slot):
        if slot < line - 1:
            return 1, (lane * (line - 1) + slot) * BODY
        return 2, lane * BODY

    def attended(tail, parts):
        cuts = []
        for lane in range(CORES):
            for slot in range(line):
                part, begin = at(lane, slot)
                middle = begin + BODY - END
                if tail:
                    cuts.append((part, middle, middle + END))
                else:
                    begin_lead = (lane * line + slot) * LEAD
                    cuts.append((0, begin_lead, begin_lead + LEAD))
                    cuts.append((part, begin, middle))
        return attend(cuts, parts, packed, origins, clip, visible, frame_counts, w_out)

    own_end, end_sent = passed_back(output(*attended(True, parts), line), table, at_place)
    parts[-1] = after(parts[-1], own_end[0])
    *terms, last = output(*attended(False, parts), line)
    own, sent = passed_back(terms + [after(last, *end_sent)], table, at_place)

    end_sums = own_end + sent_home(end_sent, table)
    end, end_feats = end_rows(current, levels, mods, head, end_sums)
    earlier = from_behind(end_feats[END - HALO :], "span", 1)
    sums = own + sent_home([after(term, end_feats) for term in sent], table)
    denoised, decoded = finish(
        current, levels, mods, head, conv_w, earlier, end, end_feats, sums
    )
    return (denoised[None], decoded[None])


def solution(mesh):
    placed = (
        P("span", "tok", None),
        P("span"),
        P(),
        P(),
        P(),
        P(None, None, "tok"),
        P(None, "tok"),
        P("tok", None),
        P(),
        P(),
    )
    return jax.shard_map(
        per_device,
        mesh=mesh,
        in_specs=placed,
        out_specs=(P("span", "tok", None), P("span", "tok", None)),
        check_vma=False,
    )
```
